512 devices in a mesh: blk: 128 (over y_hi, x, z, core), win: 4 (over y_lo).
Axes of the slice: x: 4, y: 8 (y_hi: 2, y_lo: 4; y = y_hi * 4 + y_lo), z: 8, core: 2. Of those that a mesh axis runs over, the one named last changes fastest.
Arguments:
- records: bfloat16 [8, 3, 512, 4096], P('win', None, 'blk'), may hold values from -6 to 6
- station_row: int32 [512], replicated, may hold values from 0 to 511, each once
- pair_list: int32 [4096, 2], P('blk'), may hold values from 0 to 511
- keep_mask: int32 [8, 4096], P('win', 'blk'), may hold values 0 or 1
- azimuth: float32 [2, 4096], P(None, ('blk', 'win')), may hold values from -3.140625 to 3.140625
Outputs:
- correlation: bfloat16 [4096, 9, 4096], P(('blk', 'win'))
The draws below stay inside these ranges and needn't reach their ends.
Inputs may be any that keep to these rules, and one draw needn't show every extreme that they name: `station_row`: each row index once.
All inputs are finite; a program needn't handle non-finite values. No bound on the sum of `keep_mask` on one device may be relied on, other than what follows from the above.
Results may differ from the reference program's by a relative error of at most 0.0075.
Values may be sent and summed in bfloat16 or wider, within the bound.
A program may use at most 64 MiB of HBM per device.

```python
import math
import jax
import jax.numpy as jnp
from jax import lax

PAIR_DEV = 8
NT = 4096
NF = 512
FLO = 16
SMOOTH = 11
NL = 4096
STATIONS = 512
WINDOWS = 8
P_TOT = 4096
N_BLK = 128
N_WIN = 4


def place_ends(array, rng, low, top_value):
    place = [jax.random.randint(jax.random.fold_in(rng, axis), (), 0, length) for axis, length in enumerate(array.shape)]
    widest = array.shape.index(max(array.shape))
    beside = place[:widest] + [(place[widest] + 1) % array.shape[widest]] + place[widest + 1:]
    return array.at[tuple(place)].set(low).at[tuple(beside)].set(top_value)


def level_of(key, dims, cuts, smallest, top_value):
    gain, own = 1.0, jax.random.fold_in(key, 6)
    for position, shards_of in cuts:
        draws = jnp.exp(jax.random.uniform(jax.random.fold_in(own, position), (shards_of,), jnp.float32, smallest / len(cuts), top_value / len(cuts)))
        gain = gain * jnp.repeat(draws, dims[position] // shards_of).reshape([-1 if axis == position else 1 for axis in range(len(dims))])
    return gain


def noise(stream_key, shape, width, limit, cuts=(), dtype=jnp.bfloat16):
    loudness = level_of(stream_key, shape, cuts, -0.22, 0.18) if cuts else 1.0
    entries = jax.random.normal(stream_key, shape, jnp.float32) * width * loudness
    return jnp.minimum(jnp.maximum(entries, -limit), limit).astype(dtype)


def setup_inputs(seed: int = 0) -> dict:
    keys = jax.random.split(jax.random.key(seed), 6)
    records = noise(keys[0], (WINDOWS, 3, STATIONS, NT), 1.0, 6.0, ((0, 4), (2, 128)))
    station_row = jax.random.permutation(keys[1], STATIONS).astype(jnp.int32)
    pair_list = place_ends(jax.random.randint(keys[2], (P_TOT, 2), 0, STATIONS), jax.random.fold_in(keys[2], 1), 0, STATIONS - 1).astype(jnp.int32)
    keep_mask = place_ends((jax.random.randint(keys[3], (WINDOWS, P_TOT), 0, 4) < 3).astype(jnp.int32), jax.random.fold_in(keys[3], 1), 0, 1)
    azimuth = jnp.clip(jax.random.uniform(keys[4], (2, P_TOT), jnp.float32, -3.140625, 3.140625), -3.140625, 3.140625)
    return {"records": records, "station_row": station_row, "pair_list": pair_list, "keep_mask": keep_mask, "azimuth": azimuth}


TWO_PI = 2.0 * math.pi
EPSILON = 1e-05

def forward_table(first_bin, band_bins, offset, samples, period):
    sample_ids = offset + lax.broadcasted_iota(jnp.int32, (samples, band_bins), 0)
    bin_ids = first_bin + lax.broadcasted_iota(jnp.int32, (samples, band_bins), 1)
    phase = (sample_ids * bin_ids % period).astype(jnp.float32) * (TWO_PI / period)
    return jnp.concatenate([jnp.cos(phase), -jnp.sin(phase)], axis=1).astype(jnp.bfloat16)

def inverse_table(first_bin, band_bins, lag_start, lag_count, lag_half, period):
    bin_ids = first_bin + lax.broadcasted_iota(jnp.int32, (band_bins, lag_count), 0)
    lag_ids = (lag_start + lax.broadcasted_iota(jnp.int32, (band_bins, lag_count), 1) - lag_half + period) % period
    phase = (bin_ids * lag_ids % period).astype(jnp.float32) * (TWO_PI / period)
    return jnp.concatenate([jnp.cos(phase), -jnp.sin(phase)], axis=0).astype(jnp.bfloat16)

def whiten(spectrum, band_bins, half_width):
    real_part = spectrum[..., :band_bins]
    imag_part = spectrum[..., band_bins:]
    energy = lax.optimization_barrier(jnp.sum(real_part * real_part + imag_part * imag_part, axis=1))
    smooth = energy
    for distance in range(1, half_width + 1):
        smooth = smooth + jnp.roll(energy, distance, -1) + jnp.roll(energy, -distance, -1)
    inverse_amp = lax.rsqrt(smooth / (3.0 * (2 * half_width + 1)) + EPSILON)
    both = jnp.concatenate([inverse_amp, inverse_amp], axis=-1)
    return (spectrum * both[:, None]).astype(jnp.bfloat16)

def cross_stack(first_side, second, weights, band_bins):
    first_real = first_side[..., :band_bins][:, :, :, None]
    first_imag = first_side[..., band_bins:][:, :, :, None]
    second_real = second[..., :band_bins][:, :, None]
    second_imag = second[..., band_bins:][:, :, None]
    real_part = first_real * second_real + first_imag * second_imag
    imag_part = first_imag * second_real - first_real * second_imag
    both = jnp.concatenate([real_part, imag_part], axis=-1)
    return lax.optimization_barrier(jnp.sum(both * jnp.transpose(weights)[:, :, None, None, None], axis=1))

def rotation(bearing):
    cosine = jnp.cos(bearing)
    sine_val = jnp.sin(bearing)
    filler = jnp.zeros_like(bearing)
    unity = jnp.ones_like(bearing)
    return jnp.stack([jnp.stack([sine_val, cosine, filler], -1), jnp.stack([-cosine, sine_val, filler], -1), jnp.stack([filler, filler, unity], -1)], -2)

def rotate(stacked, angles):
    rot_first = rotation(angles[0])
    rot_second = rotation(angles[1])
    return jnp.einsum('pic,pjd,pcdf->pijf', rot_first, rot_second, stacked, precision=lax.Precision.HIGHEST)

def reference(records, station_row, pair_list, keep_mask, azimuth):
    flat_rows = records.reshape(-1, NT)
    spectrum = jnp.dot(flat_rows, forward_table(FLO, NF, 0, NT, NT), preferred_element_type=jnp.float32) * (1.0 / math.sqrt(NT))
    spectrum = spectrum.reshape(WINDOWS, 3, STATIONS, 2 * NF)
    white = jnp.transpose(whiten(spectrum, NF, SMOOTH), (2, 0, 1, 3))
    lag_table = inverse_table(FLO, NF, 0, NL, NL // 2, NT)
    groups = N_BLK * N_WIN
    pair_blocks = pair_list.reshape(groups, PAIR_DEV, 2)
    keep_blocks = jnp.transpose(keep_mask.reshape(WINDOWS, groups, PAIR_DEV), (1, 0, 2))
    angle_blocks = jnp.transpose(azimuth.reshape(2, groups, PAIR_DEV), (1, 0, 2))

    def one_group(blocks_in):
        pairs_here, keep_here, angles_here = blocks_in
        first_side = jnp.take(white, jnp.take(station_row, pairs_here[:, 0]), axis=0).astype(jnp.float32)
        second = jnp.take(white, jnp.take(station_row, pairs_here[:, 1]), axis=0).astype(jnp.float32)
        stacked = cross_stack(first_side, second, keep_here.astype(jnp.float32), NF)
        rotated = rotate(stacked, angles_here).astype(jnp.bfloat16).reshape(-1, 2 * NF)
        lagged = jnp.dot(rotated, lag_table, preferred_element_type=jnp.float32) * (1.0 / math.sqrt(NF))
        return lagged.astype(jnp.bfloat16).reshape(PAIR_DEV, 9, NL)
    result = lax.map(one_group, (pair_blocks, keep_blocks, angle_blocks))
    return result.reshape(P_TOT, 9, NL)
```

```python
import math

import jax
import jax.numpy as jnp
import numpy as np
from jax import lax
from jax.experimental import pallas as pl
from jax.experimental.pallas import tpu as pltpu
from jax.sharding import PartitionSpec as P

NT = 4096
NF = 512
FLO = 16
SMOOTH = 11
NL = 4096
QUARTER = 1024
EPSILON = 1e-05

RESIDUE = (0, 0, 2, 2, 1, 1, 3, 3)
MESH = pl.DeviceIdType.MESH


def bin_order():
    place = np.arange(64)
    return np.stack([4 * ((block % 2) * 64 + place) + RESIDUE[block] for block in range(8)])


def tables():
    bins = bin_order()
    samples = np.arange(QUARTER)

    def phase(bin_ids, times):
        return (2.0 * math.pi / NT) * ((bin_ids[..., None] + FLO) * times % NT)

    ahead = phase(bins, samples)
    forward = np.concatenate([np.cos(ahead), -np.sin(ahead)], axis=1).reshape(2 * NF, QUARTER).T
    back = phase(bins, samples - NL // 2 + NT)
    back = back.reshape(8, 8, 8, QUARTER)
    inverse = np.stack([np.cos(back), -np.sin(back)], axis=2).reshape(2 * NF, QUARTER)
    flat = bins.reshape(-1)
    apart = np.abs(flat[:, None] - flat[None, :])
    near = np.minimum(apart, NF - apart) <= SMOOTH
    return (
        jnp.asarray(forward.astype(jnp.bfloat16)),
        jnp.asarray(near.astype(jnp.bfloat16)),
        jnp.asarray(inverse.astype(jnp.bfloat16)),
    )


def dot(left, right):
    return jnp.dot(left, right, preferred_element_type=jnp.float32)


def split(value):
    lead = value.astype(jnp.bfloat16).astype(jnp.float32)
    return jnp.concatenate([lead, value - lead], axis=0).astype(jnp.bfloat16)


def lanes(shape):
    return lax.broadcasted_iota(jnp.int32, shape, len(shape) - 1)


def swap_groups(vecs, group):
    vecs = list(vecs)
    lane_group = lanes(vecs[0].shape) // group
    for step in (1, 2, 4):
        high = (lane_group // step) % 2 == 1
        for i in range(8):
            if i & step:
                continue
            low_vec, high_vec = vecs[i], vecs[i + step]
            vecs[i] = jnp.where(high, pltpu.roll(high_vec, group * step, 1), low_vec)
            vecs[i + step] = jnp.where(high, high_vec, pltpu.roll(low_vec, 128 - group * step, 1))
    return vecs


def kernel(
    rec_ref, station_ref, pair_ref, keep_ref, angle_ref, fwd_hbm, near_hbm, inv_hbm, out_ref,
    rows32, fwd, near, inv, send_z, recv_z, send_x, recv_x, full, onehot,
    keep_all, info_z, info_x, send_c, recv_c, send_d, recv_d,
    tab_sem, z_s, z_r, x_s, x_r, y_s, y_r, c_s, c_r, d_s, d_r, k_s, k_r, iz_s, iz_r, ix_s, ix_r,
):
    blk = lax.axis_index("blk")
    win = lax.axis_index("win")
    y_hi, x = lax.div(blk, 64), lax.rem(lax.div(blk, 16), 4)
    z, core = lax.rem(lax.div(blk, 2), 8), lax.rem(blk, 2)
    xc, y = x * 2 + core, y_hi * 4 + win

    def at_z(k):
        other = lax.rem(z + k, 8)
        return other, (blk + (other - z) * 2, win)

    def at_x(k):
        other = lax.rem(xc + k, 8)
        return other, (y_hi * 64 + lax.div(other, 2) * 16 + z * 2 + lax.rem(other, 2), win)

    def at_y(k):
        other = lax.rem(y + k, 8)
        return other, (blk + (lax.div(other, 4) - y_hi) * 64, lax.rem(other, 4))

    def at_win(k):
        other = lax.rem(win + k, 4)
        return other, (blk, other)

    table_copies = [
        pltpu.make_async_copy(src, dst, tab_sem.at[i])
        for i, (src, dst) in enumerate(((fwd_hbm, fwd), (near_hbm, near), (inv_hbm, inv)))
    ]
    for copy in table_copies:
        copy.start()

    barrier = pltpu.get_barrier_semaphore()
    for at in (at_z, at_x, at_y):
        for k in range(1, 8):
            pl.semaphore_signal(barrier, inc=1, device_id=at(k)[1], device_id_type=MESH)

    pending = []

    def send(src, dst, sem_s, sem_r, target):
        copy = pltpu.make_async_remote_copy(
            src_ref=src, dst_ref=dst, send_sem=sem_s, recv_sem=sem_r, device_id=target, device_id_type=MESH
        )
        copy.start()
        pending.append(copy)
        return copy

    for w in range(2):
        for c in range(3):
            rows32[c * 8 + w * 4 : c * 8 + w * 4 + 4, :] = rec_ref[w, c].astype(jnp.float32)
    q0, q1, q2, q3 = [rows32[:, QUARTER * i : QUARTER * (i + 1)] for i in range(4)]
    s02, s13, d02, d13 = q0 + q2, q1 + q3, q0 - q2, q1 - q3
    left0, left2 = split(s02 + s13), split(s02 - s13)
    left1 = jnp.concatenate([split(d02), split(d13)], axis=0)

    table_copies[0].wait()
    got0 = dot(left0, fwd[:, 0:256])
    got2 = dot(left2, fwd[:, 256:512])
    got1 = dot(left1, fwd[:, 512:1024])
    even = jnp.concatenate([got0[:24] + got0[24:], got2[:24] + got2[24:]], axis=1)
    odd_a = got1[0:24] + got1[24:48]
    odd_b = got1[48:72] + got1[72:96]
    half = lanes((24, 128)) < 64
    spec = [even[:, 128 * t : 128 * t + 128] for t in range(4)]
    for t in range(4):
        turned = pltpu.roll(odd_b[:, 128 * t : 128 * t + 128], 64, 1)
        plus = half if t < 2 else jnp.logical_not(half)
        spec.append(odd_a[:, 128 * t : 128 * t + 128] + jnp.where(plus, turned, -turned))
    spec = [piece * (1.0 / math.sqrt(NT)) for piece in spec]

    half8 = lanes((8, 128)) < 64
    energy = []
    for piece in spec:
        square = piece * piece
        total = square[0:8] + square[8:16] + square[16:24]
        energy.append(total + pltpu.roll(total, 64, 1))
    energy = jnp.concatenate([jnp.where(half8, energy[2 * j], energy[2 * j + 1]) for j in range(4)], axis=1)
    table_copies[1].wait()
    smooth = dot(split(energy), near[...])
    smooth = smooth[0:8] + smooth[8:16]
    amp = lax.rsqrt(smooth / (3.0 * (2 * SMOOTH + 1)) + EPSILON)
    for t in range(8):
        piece = amp[:, 128 * (t // 2) : 128 * (t // 2) + 128]
        turned = pltpu.roll(piece, 64, 1)
        wide = jnp.where(half8, piece, turned) if t % 2 == 0 else jnp.where(half8, turned, piece)
        white = [spec[t][8 * c : 8 * c + 8] * wide for c in range(3)] + [jnp.zeros((8, 128), jnp.float32)]
        send_z[t] = jnp.concatenate(white, axis=0).astype(jnp.bfloat16)

    pl.semaphore_wait(barrier, 21)

    z_copies = []
    for k in (4, 3, 5, 2, 6, 1, 7):
        other, target = at_z(k)
        z_copies.append(send(send_z.at[other], recv_z.at[z], z_s.at[k], z_r.at[k], target))
    recv_z[z] = send_z[z]

    keep_all[win] = jnp.concatenate(
        [
            jnp.concatenate([keep_ref[...].astype(jnp.float32), jnp.zeros((2, 96), jnp.float32)], axis=1),
            jnp.zeros((6, 128), jnp.float32),
        ],
        axis=0,
    )
    k_copies = []
    for k in range(1, 4):
        k_copies.append(send(keep_all.at[win], keep_all.at[win], k_s.at[k], k_r.at[k], at_win(k)[1]))

    lane8 = lanes((8, 128))
    row8 = lax.broadcasted_iota(jnp.int32, (8, 128), 0)
    top = jnp.zeros((8, 128), jnp.float32)
    for p in range(8):
        for side in range(2):
            record = station_ref[pair_ref[win * 8 + p, side]]
            r_hi, r_x = lax.div(record, 64) // 4, lax.rem(lax.div(record, 64), 4)
            r_z, r_c, r_s = lax.rem(lax.div(record, 8), 8), lax.rem(lax.div(record, 4), 2), lax.rem(record, 4)
            place = r_hi * 256 + ((r_x * 2 + r_c) * 8 + r_z) * 4 + r_s
            spot = jnp.logical_and(row8 == side, lane8 == p)
            top = jnp.where(spot, place.astype(jnp.float32), top)
    angles = jnp.concatenate(
        [
            jnp.concatenate([angle_ref[...], jnp.zeros((2, 120), jnp.float32)], axis=1),
            jnp.zeros((6, 128), jnp.float32),
        ],
        axis=0,
    )
    sine, cosine = pltpu.roll(jnp.sin(angles), 2, 0), pltpu.roll(jnp.cos(angles), 4, 0)
    top = jnp.where(row8 < 2, top, jnp.where(row8 < 4, sine, jnp.where(row8 < 6, cosine, 0.0)))
    for copy in k_copies:
        copy.wait_recv()
    low = jnp.zeros((8, 128), jnp.float32)
    for i in range(4):
        mine = pltpu.roll(keep_all[i], lax.rem(128 - win * 8, 128), 1)
        low = low + (pltpu.roll(mine, 2 * i, 0) if i else mine)
    info_z[z] = jnp.concatenate([top, low], axis=0)
    iz_copies = []
    for k in (4, 3, 5, 2, 6, 1, 7):
        iz_copies.append(send(info_z.at[z], info_z.at[z], iz_s.at[k], iz_r.at[k], at_z(k)[1]))

    for copy in z_copies:
        copy.wait_recv()
    low_half = row8 < 4
    got = [recv_z[i].astype(jnp.float32) for i in range(8)]
    stacked = []
    for w in range(2):
        for c in range(3):
            for j in range(4):
                first, second = got[2 * j][8 * c : 8 * c + 8], got[2 * j + 1][8 * c : 8 * c + 8]
                if w == 0:
                    stacked.append(jnp.where(low_half, first, pltpu.roll(second, 4, 0)))
                else:
                    stacked.append(jnp.where(low_half, pltpu.roll(first, 4, 0), second))
    stacked += [jnp.zeros((8, 128), jnp.float32)] * 8
    turn0 = jnp.concatenate(stacked[:16], axis=0).T
    turn1 = jnp.concatenate(stacked[16:], axis=0).T
    for i in range(8):
        send_x[i] = jnp.concatenate(
            [
                jnp.concatenate([turn0[8 * i : 8 * i + 8], turn0[64 + 8 * i : 72 + 8 * i]], axis=0),
                jnp.concatenate([turn1[8 * i : 8 * i + 8], turn1[64 + 8 * i : 72 + 8 * i]], axis=0),
            ],
            axis=1,
        ).astype(jnp.bfloat16)
    x_copies = []
    for k in (4, 3, 5, 2, 6, 1, 7):
        other, target = at_x(k)
        x_copies.append(send(send_x.at[other], recv_x.at[xc], x_s.at[k], x_r.at[k], target))
    recv_x[xc] = send_x[xc]

    for copy in iz_copies:
        copy.wait_recv()
    lane16 = lanes((16, 128))
    merged = jnp.zeros((16, 128), jnp.float32)
    for i in range(8):
        piece = pltpu.roll(info_z[i], 8 * i, 1) if i else info_z[i]
        merged = jnp.where(lane16 // 8 == i, piece, merged)
    info_x[xc] = merged
    ix_copies = []
    for k in (4, 3, 5, 2, 6, 1, 7):
        ix_copies.append(send(info_x.at[xc], info_x.at[xc], ix_s.at[k], ix_r.at[k], at_x(k)[1]))

    for copy in x_copies:
        copy.wait_recv()
    got = [recv_x[i].astype(jnp.float32) for i in range(8)]
    mine = []
    for q in range(6):
        tile, group = q // 4, q % 4
        row = []
        for t in range(2):
            out = None
            for j in range(4):
                piece = got[4 * t + j][:, 128 * tile : 128 * tile + 128]
                shift = (32 * (j - group)) % 128
                piece = pltpu.roll(piece, shift, 1) if shift else piece
                out = piece if out is None else jnp.where(lane16 // 32 == j, piece, out)
            row.append(out)
        mine.append(jnp.concatenate(row, axis=1))
    full[y] = jnp.concatenate(mine, axis=0).astype(jnp.bfloat16)
    y_copies = []
    for k in (4, 3, 5, 2, 6, 1, 7):
        y_copies.append(send(full.at[y], full.at[y], y_s.at[k], y_r.at[k], at_y(k)[1]))

    for copy in ix_copies:
        copy.wait_recv()
    info = [
        jnp.where(lane16 < 64, info_x[2 * t], pltpu.roll(info_x[2 * t + 1], 64, 1)) for t in range(4)
    ]
    place_ids = lax.broadcasted_iota(jnp.int32, (256, 128), 0)
    for t in range(4):
        for side in range(2):
            place = info[t][side : side + 1].astype(jnp.int32)
            for h in range(2):
                hit = place_ids + 256 * h == place
                onehot[h, :, 256 * t + 128 * side : 256 * t + 128 * side + 128] = jnp.where(hit, 1.0, 0.0).astype(
                    jnp.bfloat16
                )

    for copy in y_copies:
        copy.wait_recv()
    c_copies = []
    low_data = full[0:4].reshape(384, 256)
    high_data = full[4:8].reshape(384, 256)
    for t in range(4):
        both = dot(low_data, onehot[0, :, 256 * t : 256 * t + 256]) + dot(
            high_data, onehot[1, :, 256 * t : 256 * t + 256]
        )
        re = [[None] * 3 for _ in range(3)]
        im = [[None] * 3 for _ in range(3)]
        for w in range(8):
            mask = jnp.broadcast_to(info[t][8 + w : 9 + w], (8, 128))
            base = 48 * w

            def part(c, ri, side):
                at = base + 16 * c + 8 * ri
                return both[at : at + 8, 128 * side : 128 * side + 128]

            first = [(part(c, 0, 0) * mask, part(c, 1, 0) * mask) for c in range(3)]
            second = [(part(c, 0, 1), part(c, 1, 1)) for c in range(3)]
            for c in range(3):
                for d in range(3):
                    ar, ai = first[c]
                    br, bi = second[d]
                    new_re, new_im = ar * br + ai * bi, ai * br - ar * bi
                    re[c][d] = new_re if w == 0 else re[c][d] + new_re
                    im[c][d] = new_im if w == 0 else im[c][d] + new_im
        s0, s1, c0, c1 = [jnp.broadcast_to(info[t][i : i + 1], (8, 128)) for i in range(2, 6)]
        for grid in (re, im):
            for d in range(3):
                e, n = grid[0][d], grid[1][d]
                grid[0][d], grid[1][d] = s0 * e + c0 * n, s0 * n - c0 * e
            for i in range(3):
                e, n = grid[i][0], grid[i][1]
                grid[i][0], grid[i][1] = s1 * e + c1 * n, s1 * n - c1 * e
        flat = []
        for i in range(3):
            for j in range(3):
                flat += [re[i][j], im[i][j]]
        main = jnp.concatenate(flat[:16], axis=0).T
        rest = jnp.concatenate(flat[16:], axis=0).T
        rest = jnp.concatenate([rest, jnp.zeros((128, 112), jnp.float32)], axis=1)
        for half_id in range(2):
            packed = jnp.zeros((8, 128), jnp.float32)
            for i in range(8):
                piece = rest[64 * half_id + 8 * i : 64 * half_id + 8 * i + 8]
                piece = pltpu.roll(piece, 16 * i, 1) if i else piece
                packed = jnp.where(lane8 // 16 == i, piece, packed)
            send_c[2 * t + half_id] = jnp.concatenate(
                [main[64 * half_id : 64 * half_id + 64], packed, jnp.zeros((8, 128), jnp.float32)], axis=0
            ).astype(jnp.bfloat16)

    for k in (4, 3, 5, 2, 6, 1, 7):
        other, target = at_x(k)
        c_copies.append(send(send_c.at[other], recv_c.at[xc], c_s.at[k], c_r.at[k], target))
    recv_c[xc] = send_c[xc]
    for copy in c_copies:
        copy.wait_recv()
    rest = swap_groups([recv_c[i, 64:80].astype(jnp.float32)[0:8] for i in range(8)], 16)
    for pair in range(4):
        pieces = [recv_c[i, 16 * pair : 16 * pair + 16].astype(jnp.float32) for i in range(8)]
        swapped = swap_groups(pieces, 16)
        for j in range(2):
            send_d[2 * pair + j] = jnp.concatenate(
                [piece[8 * j : 8 * j + 8] for piece in swapped]
                + [rest[2 * pair + j], jnp.zeros((8, 128), jnp.float32)],
                axis=0,
            ).astype(jnp.bfloat16)
    d_copies = []
    for k in (4, 3, 5, 2, 6, 1, 7):
        other, target = at_z(k)
        d_copies.append(send(send_d.at[other], recv_d.at[z], d_s.at[k], d_r.at[k], target))
    recv_d[z] = send_d[z]

    table_copies[2].wait()
    out_row = lax.broadcasted_iota(jnp.int32, (128, 80), 0)
    in_row = lax.broadcasted_iota(jnp.int32, (128, 80), 1)
    to_pair = jnp.where(
        jnp.logical_and(out_row // 16 == in_row % 8, out_row % 16 == in_row // 8), 1.0, 0.0
    ).astype(jnp.bfloat16)
    for copy in d_copies:
        copy.wait_recv()
    ordered = [dot(to_pair, recv_d[i]) for i in range(8)]
    left0 = jnp.concatenate(ordered[0:2], axis=1).astype(jnp.bfloat16)
    left2 = jnp.concatenate(ordered[2:4], axis=1).astype(jnp.bfloat16)
    at_re = lanes((128, 128)) // 8 % 2 == 0
    turned = []
    for t in range(4, 8):
        re_part, im_part = pltpu.roll(ordered[t], 8, 1), pltpu.roll(ordered[t], 120, 1)
        turned.append(jnp.where(at_re, -im_part, re_part) if t < 6 else jnp.where(at_re, im_part, -re_part))
    left1 = jnp.concatenate(
        [jnp.concatenate(ordered[4:8], axis=1), jnp.concatenate(turned, axis=1)], axis=0
    ).astype(jnp.bfloat16)
    scale = 1.0 / math.sqrt(NF)
    for n in range(4):
        cols = slice(256 * n, 256 * n + 256)
        e0 = dot(left0, inv[0:256, cols])
        e2 = dot(left2, inv[256:512, cols])
        odd = dot(left1, inv[512:1024, cols])
        plus, minus = e0 + e2, e0 - e2
        odd_p, odd_n = odd[0:128], odd[128:256]
        for i, value in enumerate((plus + odd_p, minus + odd_n, plus - odd_p, minus - odd_n)):
            value = (value * scale).astype(jnp.bfloat16)
            at = QUARTER * i + 256 * n
            for p in range(8):
                out_ref[p, :, at : at + 256] = value[16 * p : 16 * p + 9]

    for copy in pending:
        copy.wait_send()


def on_device(records, station_row, pair_list, keep_mask, azimuth):
    forward, near, inverse = tables()
    own_pairs = azimuth.shape[1]
    vmem, smem, anywhere = [
        pl.BlockSpec(memory_space=space) for space in (pltpu.VMEM, pltpu.SMEM, pl.ANY)
    ]
    bf16, f32 = jnp.bfloat16, jnp.float32
    dma = pltpu.SemaphoreType.DMA
    return pl.pallas_call(
        kernel,
        out_shape=jax.ShapeDtypeStruct((own_pairs, 9, NL), bf16),
        in_specs=[vmem, smem, smem, vmem, vmem, anywhere, anywhere, anywhere],
        out_specs=vmem,
        scratch_shapes=[
            pltpu.VMEM((24, NT), f32),
            pltpu.VMEM((QUARTER, 2 * NF), bf16),
            pltpu.VMEM((NF, NF), bf16),
            pltpu.VMEM((2 * NF, QUARTER), bf16),
            pltpu.VMEM((8, 32, 128), bf16),
            pltpu.VMEM((8, 32, 128), bf16),
            pltpu.VMEM((8, 16, 256), bf16),
            pltpu.VMEM((8, 16, 256), bf16),
            pltpu.VMEM((8, 96, 256), bf16),
            pltpu.VMEM((2, 256, 1024), bf16),
            pltpu.VMEM((4, 8, 128), f32),
            pltpu.VMEM((8, 16, 128), f32),
            pltpu.VMEM((8, 16, 128), f32),
            pltpu.VMEM((8, 80, 128), bf16),
            pltpu.VMEM((8, 80, 128), bf16),
            pltpu.VMEM((8, 80, 128), bf16),
            pltpu.VMEM((8, 80, 128), bf16),
            dma((3,)),
        ]
        + [dma((8,))] * 16,
        compiler_params=pltpu.CompilerParams(
            collective_id=0, has_side_effects=True, vmem_limit_bytes=48 << 20
        ),
        name="correlate",
    )(records, station_row, pair_list, keep_mask, azimuth, forward, near, inverse)


def solution(mesh):
    in_specs = (
        P("win", None, "blk", None),
        P(),
        P("blk", None),
        P("win", "blk"),
        P(None, ("blk", "win")),
    )
    out_specs = P(("blk", "win"), None, None)
    return jax.shard_map(
        on_device, mesh=mesh, in_specs=in_specs, out_specs=out_specs, check_vma=False
    )
```

```python
import math

import jax
import jax.numpy as jnp
import numpy as np
from jax import lax
from jax.experimental import pallas as pl
from jax.experimental.pallas import tpu as pltpu
from jax.sharding import PartitionSpec as P

NT = 4096
NF = 512
FLO = 16
SMOOTH = 11
NL = 4096
QUARTER = 1024
EPSILON = 1e-05

RESIDUE = (0, 0, 2, 2, 1, 1, 3, 3)
MESH = pl.DeviceIdType.MESH


def bin_order():
    place = np.arange(64)
    return np.stack([4 * ((block % 2) * 64 + place) + RESIDUE[block] for block in range(8)])


def tables():
    bins = bin_order()
    samples = np.arange(QUARTER)

    def phase(bin_ids, times):
        return (2.0 * math.pi / NT) * ((bin_ids[..., None] + FLO) * times % NT)

    ahead = phase(bins, samples)
    forward = np.concatenate([np.cos(ahead), -np.sin(ahead)], axis=1).reshape(2 * NF, QUARTER).T
    back = phase(bins, samples - NL // 2 + NT)
    back = back.reshape(8, 8, 8, QUARTER)
    inverse = np.stack([np.cos(back), -np.sin(back)], axis=2).reshape(2 * NF, QUARTER)
    flat = bins.reshape(-1)
    apart = np.abs(flat[:, None] - flat[None, :])
    near = np.minimum(apart, NF - apart) <= SMOOTH
    return (
        jnp.asarray(forward.astype(jnp.bfloat16)),
        jnp.asarray(near.astype(jnp.bfloat16)),
        jnp.asarray(inverse.astype(jnp.bfloat16)),
    )


def dot(left, right):
    return jnp.dot(left, right, preferred_element_type=jnp.float32)


def split(value):
    lead = value.astype(jnp.bfloat16).astype(jnp.float32)
    return jnp.concatenate([lead, value - lead], axis=0).astype(jnp.bfloat16)


def lanes(shape):
    return lax.broadcasted_iota(jnp.int32, shape, len(shape) - 1)


def swap_groups(vecs, group):
    vecs = list(vecs)
    lane_group = lanes(vecs[0].shape) // group
    for step in (1, 2, 4):
        high = (lane_group // step) % 2 == 1
        for i in range(8):
            if i & step:
                continue
            low_vec, high_vec = vecs[i], vecs[i + step]
            vecs[i] = jnp.where(high, pltpu.roll(high_vec, group * step, 1), low_vec)
            vecs[i + step] = jnp.where(high, high_vec, pltpu.roll(low_vec, 128 - group * step, 1))
    return vecs


def kernel(
    rec_hbm, station_hbm, pair_hbm, keep_hbm, angle_hbm, fwd_hbm, near_hbm, inv_hbm, out_ref,
    rec_ref, station_ref, pair_ref, keep_ref, angle_ref,
    rows32, fwd, near, inv, send_z, recv_z, send_x, recv_x, full, onehot,
    keep_all, info_z, info_x, send_c, recv_c, send_d, recv_d,
    tab_sem, z_s, z_r, x_s, x_r, y_s, y_r, c_s, c_r, d_s, d_r, k_s, k_r, iz_s, iz_r, ix_s, ix_r,
):
    blk = lax.axis_index("blk")
    win = lax.axis_index("win")
    y_hi, x = lax.div(blk, 64), lax.rem(lax.div(blk, 16), 4)
    z, core = lax.rem(lax.div(blk, 2), 8), lax.rem(blk, 2)
    xc, y = x * 2 + core, y_hi * 4 + win

    def at_z(k):
        other = lax.rem(z + k, 8)
        return other, (blk + (other - z) * 2, win)

    def at_x(k):
        other = lax.rem(xc + k, 8)
        return other, (y_hi * 64 + lax.div(other, 2) * 16 + z * 2 + lax.rem(other, 2), win)

    def at_y(k):
        other = lax.rem(y + k, 8)
        return other, (blk + (lax.div(other, 4) - y_hi) * 64, lax.rem(other, 4))

    def at_win(k):
        other = lax.rem(win + k, 4)
        return other, (blk, other)

    loads = [
        pltpu.make_async_copy(src, dst, tab_sem.at[i])
        for i, (src, dst) in enumerate(
            (
                (rec_hbm, rec_ref),
                (fwd_hbm, fwd),
                (near_hbm, near),
                (keep_hbm, keep_ref),
                (station_hbm, station_ref),
                (pair_hbm, pair_ref),
                (angle_hbm, angle_ref),
                (inv_hbm, inv),
            )
        )
    ]
    for copy in loads:
        copy.start()

    barrier = pltpu.get_barrier_semaphore()
    for at in (at_z, at_x, at_y):
        for k in range(1, 8):
            pl.semaphore_signal(barrier, inc=1, device_id=at(k)[1], device_id_type=MESH)

    pending = []

    def send(src, dst, sem_s, sem_r, target):
        copy = pltpu.make_async_remote_copy(
            src_ref=src, dst_ref=dst, send_sem=sem_s, recv_sem=sem_r, device_id=target, device_id_type=MESH
        )
        copy.start()
        pending.append(copy)
        return copy

    loads[0].wait()
    for w in range(2):
        for c in range(3):
            rows32[c * 8 + w * 4 : c * 8 + w * 4 + 4, :] = rec_ref[w, c].astype(jnp.float32)
    q0, q1, q2, q3 = [rows32[:, QUARTER * i : QUARTER * (i + 1)] for i in range(4)]
    s02, s13, d02, d13 = q0 + q2, q1 + q3, q0 - q2, q1 - q3
    left0, left2 = split(s02 + s13), split(s02 - s13)
    left1 = jnp.concatenate([split(d02), split(d13)], axis=0)

    loads[1].wait()
    got0 = dot(left0, fwd[:, 0:256])
    got2 = dot(left2, fwd[:, 256:512])
    got1 = dot(left1, fwd[:, 512:1024])
    even = jnp.concatenate([got0[:24] + got0[24:], got2[:24] + got2[24:]], axis=1)
    odd_a = got1[0:24] + got1[24:48]
    odd_b = got1[48:72] + got1[72:96]
    half = lanes((24, 128)) < 64
    spec = [even[:, 128 * t : 128 * t + 128] for t in range(4)]
    for t in range(4):
        turned = pltpu.roll(odd_b[:, 128 * t : 128 * t + 128], 64, 1)
        plus = half if t < 2 else jnp.logical_not(half)
        spec.append(odd_a[:, 128 * t : 128 * t + 128] + jnp.where(plus, turned, -turned))
    spec = [piece * (1.0 / math.sqrt(NT)) for piece in spec]

    half8 = lanes((8, 128)) < 64
    energy = []
    for piece in spec:
        square = piece * piece
        total = square[0:8] + square[8:16] + square[16:24]
        energy.append(total + pltpu.roll(total, 64, 1))
    energy = jnp.concatenate([jnp.where(half8, energy[2 * j], energy[2 * j + 1]) for j in range(4)], axis=1)
    loads[2].wait()
    smooth = dot(split(energy), near[...])
    smooth = smooth[0:8] + smooth[8:16]
    amp = lax.rsqrt(smooth / (3.0 * (2 * SMOOTH + 1)) + EPSILON)
    for t in range(8):
        piece = amp[:, 128 * (t // 2) : 128 * (t // 2) + 128]
        turned = pltpu.roll(piece, 64, 1)
        wide = jnp.where(half8, piece, turned) if t % 2 == 0 else jnp.where(half8, turned, piece)
        white = [spec[t][8 * c : 8 * c + 8] * wide for c in range(3)] + [jnp.zeros((8, 128), jnp.float32)]
        send_z[t] = jnp.concatenate(white, axis=0).astype(jnp.bfloat16)

    pl.semaphore_wait(barrier, 21)

    z_copies = []
    for k in (4, 3, 5, 2, 6, 1, 7):
        other, target = at_z(k)
        z_copies.append(send(send_z.at[other], recv_z.at[z], z_s.at[k], z_r.at[k], target))
    recv_z[z] = send_z[z]

    loads[3].wait()
    keep_all[win] = jnp.concatenate(
        [
            jnp.concatenate([keep_ref[...].astype(jnp.float32), jnp.zeros((2, 96), jnp.float32)], axis=1),
            jnp.zeros((6, 128), jnp.float32),
        ],
        axis=0,
    )
    k_copies = []
    for k in range(1, 4):
        k_copies.append(send(keep_all.at[win], keep_all.at[win], k_s.at[k], k_r.at[k], at_win(k)[1]))

    for copy in loads[4:7]:
        copy.wait()
    lane8 = lanes((8, 128))
    row8 = lax.broadcasted_iota(jnp.int32, (8, 128), 0)
    top = jnp.zeros((8, 128), jnp.float32)
    for p in range(8):
        for side in range(2):
            record = station_ref[pair_ref[side, win * 8 + p]]
            r_hi, r_x = lax.div(record, 64) // 4, lax.rem(lax.div(record, 64), 4)
            r_z, r_c, r_s = lax.rem(lax.div(record, 8), 8), lax.rem(lax.div(record, 4), 2), lax.rem(record, 4)
            place = r_hi * 256 + ((r_x * 2 + r_c) * 8 + r_z) * 4 + r_s
            spot = jnp.logical_and(row8 == side, lane8 == p)
            top = jnp.where(spot, place.astype(jnp.float32), top)
    angles = jnp.concatenate(
        [
            jnp.concatenate([angle_ref[...], jnp.zeros((2, 120), jnp.float32)], axis=1),
            jnp.zeros((6, 128), jnp.float32),
        ],
        axis=0,
    )
    sine, cosine = pltpu.roll(jnp.sin(angles), 2, 0), pltpu.roll(jnp.cos(angles), 4, 0)
    top = jnp.where(row8 < 2, top, jnp.where(row8 < 4, sine, jnp.where(row8 < 6, cosine, 0.0)))
    for copy in k_copies:
        copy.wait_recv()
    low = jnp.zeros((8, 128), jnp.float32)
    for i in range(4):
        mine = pltpu.roll(keep_all[i], lax.rem(128 - win * 8, 128), 1)
        low = low + (pltpu.roll(mine, 2 * i, 0) if i else mine)
    info_z[z] = jnp.concatenate([top, low], axis=0)
    iz_copies = []
    for k in (4, 3, 5, 2, 6, 1, 7):
        iz_copies.append(send(info_z.at[z], info_z.at[z], iz_s.at[k], iz_r.at[k], at_z(k)[1]))

    for copy in z_copies:
        copy.wait_recv()
    low_half = row8 < 4
    got = [recv_z[i].astype(jnp.float32) for i in range(8)]
    stacked = []
    for w in range(2):
        for c in range(3):
            for j in range(4):
                first, second = got[2 * j][8 * c : 8 * c + 8], got[2 * j + 1][8 * c : 8 * c + 8]
                if w == 0:
                    stacked.append(jnp.where(low_half, first, pltpu.roll(second, 4, 0)))
                else:
                    stacked.append(jnp.where(low_half, pltpu.roll(first, 4, 0), second))
    stacked += [jnp.zeros((8, 128), jnp.float32)] * 8
    turn0 = jnp.concatenate(stacked[:16], axis=0).T
    turn1 = jnp.concatenate(stacked[16:], axis=0).T
    for i in range(8):
        send_x[i] = jnp.concatenate(
            [
                jnp.concatenate([turn0[8 * i : 8 * i + 8], turn0[64 + 8 * i : 72 + 8 * i]], axis=0),
                jnp.concatenate([turn1[8 * i : 8 * i + 8], turn1[64 + 8 * i : 72 + 8 * i]], axis=0),
            ],
            axis=1,
        ).astype(jnp.bfloat16)
    x_copies = []
    for k in (4, 3, 5, 2, 6, 1, 7):
        other, target = at_x(k)
        x_copies.append(send(send_x.at[other], recv_x.at[xc], x_s.at[k], x_r.at[k], target))
    recv_x[xc] = send_x[xc]

    for copy in iz_copies:
        copy.wait_recv()
    lane16 = lanes((16, 128))
    merged = jnp.zeros((16, 128), jnp.float32)
    for i in range(8):
        piece = pltpu.roll(info_z[i], 8 * i, 1) if i else info_z[i]
        merged = jnp.where(lane16 // 8 == i, piece, merged)
    info_x[xc] = merged
    ix_copies = []
    for k in (4, 3, 5, 2, 6, 1, 7):
        ix_copies.append(send(info_x.at[xc], info_x.at[xc], ix_s.at[k], ix_r.at[k], at_x(k)[1]))

    for copy in x_copies:
        copy.wait_recv()
    got = [recv_x[i].astype(jnp.float32) for i in range(8)]
    mine = []
    for q in range(6):
        tile, group = q // 4, q % 4
        row = []
        for t in range(2):
            out = None
            for j in range(4):
                piece = got[4 * t + j][:, 128 * tile : 128 * tile + 128]
                shift = (32 * (j - group)) % 128
                piece = pltpu.roll(piece, shift, 1) if shift else piece
                out = piece if out is None else jnp.where(lane16 // 32 == j, piece, out)
            row.append(out)
        mine.append(jnp.concatenate(row, axis=1))
    full[y] = jnp.concatenate(mine, axis=0).astype(jnp.bfloat16)
    y_copies = []
    for k in (4, 3, 5, 2, 6, 1, 7):
        y_copies.append(send(full.at[y], full.at[y], y_s.at[k], y_r.at[k], at_y(k)[1]))

    for copy in ix_copies:
        copy.wait_recv()
    info = [
        jnp.where(lane16 < 64, info_x[2 * t], pltpu.roll(info_x[2 * t + 1], 64, 1)) for t in range(4)
    ]
    place_ids = lax.broadcasted_iota(jnp.int32, (256, 128), 0)
    for t in range(4):
        for side in range(2):
            place = info[t][side : side + 1].astype(jnp.int32)
            for h in range(2):
                hit = place_ids + 256 * h == place
                onehot[h, :, 256 * t + 128 * side : 256 * t + 128 * side + 128] = jnp.where(hit, 1.0, 0.0).astype(
                    jnp.bfloat16
                )

    for copy in y_copies:
        copy.wait_recv()
    c_copies = []
    low_data = full[0:4].reshape(384, 256)
    high_data = full[4:8].reshape(384, 256)
    for t in range(4):
        both = dot(low_data, onehot[0, :, 256 * t : 256 * t + 256]) + dot(
            high_data, onehot[1, :, 256 * t : 256 * t + 256]
        )
        re = [[None] * 3 for _ in range(3)]
        im = [[None] * 3 for _ in range(3)]
        for w in range(8):
            mask = jnp.broadcast_to(info[t][8 + w : 9 + w], (8, 128))
            base = 48 * w

            def part(c, ri, side):
                at = base + 16 * c + 8 * ri
                return both[at : at + 8, 128 * side : 128 * side + 128]

            first = [(part(c, 0, 0) * mask, part(c, 1, 0) * mask) for c in range(3)]
            second = [(part(c, 0, 1), part(c, 1, 1)) for c in range(3)]
            for c in range(3):
                for d in range(3):
                    ar, ai = first[c]
                    br, bi = second[d]
                    new_re, new_im = ar * br + ai * bi, ai * br - ar * bi
                    re[c][d] = new_re if w == 0 else re[c][d] + new_re
                    im[c][d] = new_im if w == 0 else im[c][d] + new_im
        s0, s1, c0, c1 = [jnp.broadcast_to(info[t][i : i + 1], (8, 128)) for i in range(2, 6)]
        for grid in (re, im):
            for d in range(3):
                e, n = grid[0][d], grid[1][d]
                grid[0][d], grid[1][d] = s0 * e + c0 * n, s0 * n - c0 * e
            for i in range(3):
                e, n = grid[i][0], grid[i][1]
                grid[i][0], grid[i][1] = s1 * e + c1 * n, s1 * n - c1 * e
        flat = []
        for i in range(3):
            for j in range(3):
                flat += [re[i][j], im[i][j]]
        main = jnp.concatenate(flat[:16], axis=0).T
        rest = jnp.concatenate(flat[16:], axis=0).T
        rest = jnp.concatenate([rest, jnp.zeros((128, 112), jnp.float32)], axis=1)
        for half_id in range(2):
            packed = jnp.zeros((8, 128), jnp.float32)
            for i in range(8):
                piece = rest[64 * half_id + 8 * i : 64 * half_id + 8 * i + 8]
                piece = pltpu.roll(piece, 16 * i, 1) if i else piece
                packed = jnp.where(lane8 // 16 == i, piece, packed)
            send_c[2 * t + half_id] = jnp.concatenate(
                [main[64 * half_id : 64 * half_id + 64], packed, jnp.zeros((8, 128), jnp.float32)], axis=0
            ).astype(jnp.bfloat16)

    for k in (4, 3, 5, 2, 6, 1, 7):
        other, target = at_x(k)
        c_copies.append(send(send_c.at[other], recv_c.at[xc], c_s.at[k], c_r.at[k], target))
    recv_c[xc] = send_c[xc]
    for copy in c_copies:
        copy.wait_recv()
    rest = swap_groups([recv_c[i, 64:80].astype(jnp.float32)[0:8] for i in range(8)], 16)
    for pair in range(4):
        pieces = [recv_c[i, 16 * pair : 16 * pair + 16].astype(jnp.float32) for i in range(8)]
        swapped = swap_groups(pieces, 16)
        for j in range(2):
            send_d[2 * pair + j] = jnp.concatenate(
                [piece[8 * j : 8 * j + 8] for piece in swapped]
                + [rest[2 * pair + j], jnp.zeros((8, 128), jnp.float32)],
                axis=0,
            ).astype(jnp.bfloat16)
    d_copies = []
    for k in (4, 3, 5, 2, 6, 1, 7):
        other, target = at_z(k)
        d_copies.append(send(send_d.at[other], recv_d.at[z], d_s.at[k], d_r.at[k], target))
    recv_d[z] = send_d[z]

    loads[7].wait()
    for copy in d_copies:
        copy.wait_recv()
    ordered = [recv_d[i].astype(jnp.float32) for i in range(8)]
    left0 = jnp.concatenate(ordered[0:2], axis=1).astype(jnp.bfloat16)
    left2 = jnp.concatenate(ordered[2:4], axis=1).astype(jnp.bfloat16)
    at_re = lanes((80, 128)) // 8 % 2 == 0
    turned = []
    for t in range(4, 8):
        re_part, im_part = pltpu.roll(ordered[t], 8, 1), pltpu.roll(ordered[t], 120, 1)
        turned.append(jnp.where(at_re, -im_part, re_part) if t < 6 else jnp.where(at_re, im_part, -re_part))
    left1 = jnp.concatenate(
        [jnp.concatenate(ordered[4:8], axis=1), jnp.concatenate(turned, axis=1)], axis=0
    ).astype(jnp.bfloat16)
    scale = 1.0 / math.sqrt(NF)
    for n in range(4):
        cols = slice(256 * n, 256 * n + 256)
        e0 = dot(left0, inv[0:256, cols])
        e2 = dot(left2, inv[256:512, cols])
        odd = dot(left1, inv[512:1024, cols])
        plus, minus = e0 + e2, e0 - e2
        odd_p, odd_n = odd[0:80], odd[80:160]
        for i, value in enumerate((plus + odd_p, minus + odd_n, plus - odd_p, minus - odd_n)):
            value = (value[0:72] * scale).reshape(9, 8, 256).astype(jnp.bfloat16)
            at = QUARTER * i + 256 * n
            out_ref[:, :, at : at + 256] = value

    for copy in pending:
        copy.wait_send()


def on_device(records, station_row, pair_list, keep_mask, azimuth):
    forward, near, inverse = tables()
    own_pairs = azimuth.shape[1]
    bf16, f32 = jnp.bfloat16, jnp.float32
    dma = pltpu.SemaphoreType.DMA
    lagged = pl.pallas_call(
        kernel,
        out_shape=jax.ShapeDtypeStruct((9, own_pairs, NL), bf16),
        in_specs=[pl.BlockSpec(memory_space=pltpu.HBM)] * 8,
        out_specs=pl.BlockSpec(memory_space=pltpu.VMEM),
        scratch_shapes=[
            pltpu.VMEM(records.shape, bf16),
            pltpu.SMEM(station_row.shape, jnp.int32),
            pltpu.SMEM(pair_list.shape[::-1], jnp.int32),
            pltpu.VMEM(keep_mask.shape, jnp.int32),
            pltpu.VMEM(azimuth.shape, f32),
            pltpu.VMEM((24, NT), f32),
            pltpu.VMEM((QUARTER, 2 * NF), bf16),
            pltpu.VMEM((NF, NF), bf16),
            pltpu.VMEM((2 * NF, QUARTER), bf16),
            pltpu.VMEM((8, 32, 128), bf16),
            pltpu.VMEM((8, 32, 128), bf16),
            pltpu.VMEM((8, 16, 256), bf16),
            pltpu.VMEM((8, 16, 256), bf16),
            pltpu.VMEM((8, 96, 256), bf16),
            pltpu.VMEM((2, 256, 1024), bf16),
            pltpu.VMEM((4, 8, 128), f32),
            pltpu.VMEM((8, 16, 128), f32),
            pltpu.VMEM((8, 16, 128), f32),
            pltpu.VMEM((8, 80, 128), bf16),
            pltpu.VMEM((8, 80, 128), bf16),
            pltpu.VMEM((8, 80, 128), bf16),
            pltpu.VMEM((8, 80, 128), bf16),
            dma((8,)),
        ]
        + [dma((8,))] * 16,
        compiler_params=pltpu.CompilerParams(
            collective_id=0, has_side_effects=True, vmem_limit_bytes=48 << 20
        ),
        name="correlate",
    )(
        *[
            pltpu.with_memory_space_constraint(operand, pltpu.HBM)
            for operand in (records, station_row, pair_list.T, keep_mask, azimuth, forward, near, inverse)
        ]
    )
    return jnp.transpose(lagged, (1, 0, 2))


def solution(mesh):
    in_specs = (
        P("win", None, "blk", None),
        P(),
        P("blk", None),
        P("win", "blk"),
        P(None, ("blk", "win")),
    )
    out_specs = P(("blk", "win"), None, None)
    return jax.shard_map(
        on_device, mesh=mesh, in_specs=in_specs, out_specs=out_specs, check_vma=False
    )
```

```python
import math

import jax
import jax.numpy as jnp
import numpy as np
from jax import lax
from jax.experimental import pallas as pl
from jax.experimental.pallas import tpu as pltpu
from jax.sharding import PartitionSpec as P

NT = 4096
NF = 512
FLO = 16
SMOOTH = 11
NL = 4096
QUARTER = 1024
EPSILON = 1e-05

RESIDUE = (0, 0, 2, 2, 1, 1, 3, 3)
MESH = pl.DeviceIdType.MESH


def bin_order():
    place = np.arange(64)
    return np.stack([4 * ((block % 2) * 64 + place) + RESIDUE[block] for block in range(8)])


def tables():
    bins = bin_order()
    samples = np.arange(QUARTER)

    def phase(bin_ids, times):
        return (2.0 * math.pi / NT) * ((bin_ids[..., None] + FLO) * times % NT)

    ahead = phase(bins, samples)
    forward = np.concatenate([np.cos(ahead), -np.sin(ahead)], axis=1).reshape(2 * NF, QUARTER).T
    back = phase(bins, samples - NL // 2 + NT)
    back = back.reshape(8, 8, 8, QUARTER)
    inverse = np.stack([np.cos(back), -np.sin(back)], axis=2).reshape(2 * NF, QUARTER)
    flat = bins.reshape(-1)
    apart = np.abs(flat[:, None] - flat[None, :])
    near = np.minimum(apart, NF - apart) <= SMOOTH
    return (
        jnp.asarray(forward.astype(jnp.bfloat16)),
        jnp.asarray(near.astype(jnp.bfloat16)),
        jnp.asarray(inverse.astype(jnp.bfloat16)),
    )


def dot(left, right):
    return jnp.dot(left, right, preferred_element_type=jnp.float32)


def split(value):
    lead = value.astype(jnp.bfloat16).astype(jnp.float32)
    return jnp.concatenate([lead, value - lead], axis=0).astype(jnp.bfloat16)


def lanes(shape):
    return lax.broadcasted_iota(jnp.int32, shape, len(shape) - 1)


def swap_groups(vecs, group):
    vecs = list(vecs)
    lane_group = lanes(vecs[0].shape) // group
    for step in (1, 2, 4):
        high = (lane_group // step) % 2 == 1
        for i in range(8):
            if i & step:
                continue
            low_vec, high_vec = vecs[i], vecs[i + step]
            vecs[i] = jnp.where(high, pltpu.roll(high_vec, group * step, 1), low_vec)
            vecs[i + step] = jnp.where(high, high_vec, pltpu.roll(low_vec, 128 - group * step, 1))
    return vecs


def kernel(
    rec_hbm, station_hbm, pair_hbm, keep_hbm, angle_hbm, fwd_hbm, near_hbm, inv_hbm, out_ref,
    rec_ref, station_ref, pair_ref, keep_ref, angle_ref,
    rows32, fwd, near, inv, send_z, recv_z, send_x, recv_x, full, onehot,
    send_k, recv_k, send_c, recv_c, send_d, recv_d,
    tab_sem, z_s, z_r, x_s, x_r, y_s, y_r, c_s, c_r, d_s, d_r, k_s, k_r,
):
    blk = lax.axis_index("blk")
    win = lax.axis_index("win")
    y_hi, x = lax.div(blk, 64), lax.rem(lax.div(blk, 16), 4)
    z, core = lax.rem(lax.div(blk, 2), 8), lax.rem(blk, 2)
    xc, y = x * 2 + core, y_hi * 4 + win

    at_z, at_x, at_y, at_win = [None], [None], [None], [None]
    for k in range(1, 8):
        other = lax.rem(z + k, 8)
        at_z.append((other, (blk + (other - z) * 2, win)))
        other = lax.rem(xc + k, 8)
        at_x.append((other, (y_hi * 64 + lax.div(other, 2) * 16 + z * 2 + lax.rem(other, 2), win)))
        other = lax.rem(y + k, 8)
        at_y.append((other, (blk + (lax.div(other, 4) - y_hi) * 64, lax.rem(other, 4))))
    for k in range(1, 4):
        other = lax.rem(win + k, 4)
        at_win.append((other, (blk, other)))

    loads = [
        pltpu.make_async_copy(src, dst, tab_sem.at[i])
        for i, (src, dst) in enumerate(
            (
                (rec_hbm, rec_ref),
                (fwd_hbm, fwd),
                (near_hbm, near),
                (keep_hbm, keep_ref),
                (station_hbm, station_ref),
                (pair_hbm, pair_ref),
                (angle_hbm, angle_ref),
                (inv_hbm, inv),
            )
        )
    ]
    for copy in loads[:7]:
        copy.start()

    barrier = pltpu.get_barrier_semaphore()
    for at in (at_z, at_x, at_y):
        for k in range(1, 8):
            pl.semaphore_signal(barrier, inc=1, device_id=at[k][1], device_id_type=MESH)

    pending = []

    def send(src, dst, sem_s, sem_r, target):
        copy = pltpu.make_async_remote_copy(
            src_ref=src, dst_ref=dst, send_sem=sem_s, recv_sem=sem_r, device_id=target, device_id_type=MESH
        )
        copy.start()
        pending.append(copy)
        return copy

    for copy in loads[3:6]:
        copy.wait()
    lane8, lane16 = lanes((8, 128)), lanes((16, 128))
    row8 = lax.broadcasted_iota(jnp.int32, (8, 128), 0)
    row16 = lax.broadcasted_iota(jnp.int32, (16, 128), 0)
    zero8 = jnp.zeros((8, 128), jnp.float32)
    record = jnp.zeros((8, 128), jnp.int32)
    for p in range(8):
        for side in range(2):
            spot = jnp.logical_and(row8 == side, lane8 == p)
            record = jnp.where(spot, station_ref[pair_ref[side, win * 8 + p]], record)
    r_hi, r_x, r_z = record // 256, record // 64 % 4, record // 8 % 8
    r_c, r_s = record // 4 % 2, record % 4
    place = r_hi * 256 + ((r_x * 2 + r_c) * 8 + r_z) * 4 + r_s
    first_digit = (place // 16).astype(jnp.float32)
    second_digit = (place % 16).astype(jnp.float32)
    keep = jnp.concatenate([keep_ref[...].astype(jnp.float32), jnp.zeros((2, 96), jnp.float32)], axis=1)
    keep = jnp.concatenate([keep, jnp.zeros((6, 128), jnp.float32)], axis=0)
    own_table = jnp.where(
        row8 < 2, first_digit, jnp.where(row8 < 4, pltpu.roll(second_digit, 2, 0), pltpu.roll(keep, 4, 0))
    )

    loads[0].wait()
    for w in range(2):
        for c in range(3):
            rows32[c * 8 + w * 4 : c * 8 + w * 4 + 4, :] = rec_ref[w, c].astype(jnp.float32)
    q0, q1, q2, q3 = [rows32[:, QUARTER * i : QUARTER * (i + 1)] for i in range(4)]
    s02, s13, d02, d13 = q0 + q2, q1 + q3, q0 - q2, q1 - q3
    left0, left2 = split(s02 + s13), split(s02 - s13)
    left1 = jnp.concatenate([split(d02), split(d13)], axis=0)

    loads[1].wait()
    got0 = dot(left0, fwd[:, 0:256])
    got2 = dot(left2, fwd[:, 256:512])
    got1 = dot(left1, fwd[:, 512:1024])
    even = jnp.concatenate([got0[:24] + got0[24:], got2[:24] + got2[24:]], axis=1)
    odd_a = got1[0:24] + got1[24:48]
    odd_b = got1[48:72] + got1[72:96]
    half = lanes((24, 128)) < 64
    spec = [even[:, 128 * t : 128 * t + 128] for t in range(4)]
    for t in range(4):
        turned = pltpu.roll(odd_b[:, 128 * t : 128 * t + 128], 64, 1)
        plus = half if t < 2 else jnp.logical_not(half)
        spec.append(odd_a[:, 128 * t : 128 * t + 128] + jnp.where(plus, turned, -turned))
    spec = [piece * (1.0 / math.sqrt(NT)) for piece in spec]

    half8 = lanes((8, 128)) < 64
    energy = []
    for piece in spec:
        square = piece * piece
        total = square[0:8] + square[8:16] + square[16:24]
        energy.append(total + pltpu.roll(total, 64, 1))
    energy = jnp.concatenate([jnp.where(half8, energy[2 * j], energy[2 * j + 1]) for j in range(4)], axis=1)
    loads[2].wait()
    smooth = dot(split(energy), near[...])
    smooth = smooth[0:8] + smooth[8:16]
    amp = lax.rsqrt(smooth / (3.0 * (2 * SMOOTH + 1)) + EPSILON)
    for t in range(8):
        piece = amp[:, 128 * (t // 2) : 128 * (t // 2) + 128]
        turned = pltpu.roll(piece, 64, 1)
        wide = jnp.where(half8, piece, turned) if t % 2 == 0 else jnp.where(half8, turned, piece)
        white = [spec[t][8 * c : 8 * c + 8] * wide for c in range(3)] + [own_table]
        send_z[t] = jnp.concatenate(white, axis=0).astype(jnp.bfloat16)

    pl.semaphore_wait(barrier, 21)

    z_copies = []
    for k in (4, 3, 5, 2, 6, 1, 7):
        other, target = at_z[k]
        z_copies.append(send(send_z.at[other], recv_z.at[z], z_s.at[k], z_r.at[k], target))
    recv_z[z] = send_z[z]

    loads[7].start()

    for copy in z_copies:
        copy.wait_recv()
    low_half = row8 < 4
    got = [recv_z[i].astype(jnp.float32) for i in range(8)]
    stacked = []
    for w in range(2):
        for c in range(3):
            for j in range(4):
                first, second = got[2 * j][8 * c : 8 * c + 8], got[2 * j + 1][8 * c : 8 * c + 8]
                if w == 0:
                    stacked.append(jnp.where(low_half, first, pltpu.roll(second, 4, 0)))
                else:
                    stacked.append(jnp.where(low_half, pltpu.roll(first, 4, 0), second))
    stacked += [zero8] * 8
    table = []
    for q in range(4):
        merged = zero8
        for i in range(8):
            piece = pltpu.roll(got[i][24:32], (64 + 8 * i - 8 * q) % 128, 1)
            merged = jnp.where(lane8 // 8 == 8 + i, piece, merged)
        table.append(merged)
    tail = jnp.concatenate(
        [
            jnp.where(row8 < 6, table[0], pltpu.roll(table[1], 2, 0)),
            jnp.where(row8 < 2, pltpu.roll(table[2], 4, 0), jnp.where(row8 < 4, pltpu.roll(table[3], 6, 0), 0.0)),
        ],
        axis=0,
    )
    turn0 = jnp.concatenate(stacked[:16], axis=0).T
    turn1 = jnp.concatenate(stacked[16:], axis=0).T
    for i in range(8):
        send_x[i] = jnp.concatenate(
            [
                jnp.concatenate([turn0[8 * i : 8 * i + 8], turn0[64 + 8 * i : 72 + 8 * i]], axis=0),
                jnp.concatenate([turn1[8 * i : 8 * i + 8], turn1[64 + 8 * i : 72 + 8 * i]], axis=0) + tail,
            ],
            axis=1,
        ).astype(jnp.bfloat16)
    x_copies = []
    for k in (4, 3, 5, 2, 6, 1, 7):
        other, target = at_x[k]
        x_copies.append(send(send_x.at[other], recv_x.at[xc], x_s.at[k], x_r.at[k], target))
    recv_x[xc] = send_x[xc]

    for copy in x_copies:
        copy.wait_recv()
    got = [recv_x[i].astype(jnp.float32) for i in range(8)]
    mine = []
    for q in range(6):
        tile, group = q // 4, q % 4
        row = []
        for t in range(2):
            out = None
            for j in range(4):
                piece = got[4 * t + j][:, 128 * tile : 128 * tile + 128]
                shift = (32 * (j - group)) % 128
                piece = pltpu.roll(piece, shift, 1) if shift else piece
                out = piece if out is None else jnp.where(lane16 // 32 == j, piece, out)
            row.append(out)
        mine.append(jnp.concatenate(row, axis=1))
    full[y] = jnp.concatenate(mine, axis=0).astype(jnp.bfloat16)
    info = [
        jnp.where(lane16 < 64, pltpu.roll(got[2 * t][:, 128:256], 64, 1), got[2 * t + 1][:, 128:256])
        for t in range(4)
    ]
    def share(source, h, k, sem):
        block = full.at[source, pl.ds(48 * h, 48)]
        return send(block, block, y_s.at[sem], y_r.at[sem], at_y[k][1])

    direct = {}
    for k in (2, 6, 1, 7):
        for h in range(2):
            direct[k, h] = share(y, h, k, len(direct))
    y_copies = [direct[1, 0], direct[1, 1], direct[7, 0], direct[7, 1]]
    for q in range(4):
        masks = jnp.zeros((16, 128), jnp.float32)
        for t in range(4):
            shift = (2 * t - 4 - 2 * q) % 16
            piece = pltpu.roll(info[t], shift, 0) if shift else info[t]
            masks = jnp.where(row16 // 2 == t, piece, masks)
        send_k[q] = masks.astype(jnp.bfloat16)
    for k in range(1, 4):
        other, target = at_win[k]
        y_copies.append(send(send_k.at[other], recv_k.at[win], k_s.at[k], k_r.at[k], target))
    recv_k[win] = send_k[win]
    place_ids = lax.broadcasted_iota(jnp.int32, (256, 128), 0)
    for t in range(4):
        for side in range(2):
            place = (16.0 * info[t][side : side + 1] + info[t][2 + side : 3 + side]).astype(jnp.int32)
            for h in range(2):
                hit = place_ids + 256 * h == place
                onehot[h, :, 256 * t + 128 * side : 256 * t + 128 * side + 128] = jnp.where(hit, 1.0, 0.0).astype(
                    jnp.bfloat16
                )

    for h in range(2):
        for step, (k, near_k) in enumerate(((2, 1), (6, 7))):
            direct[k, h].wait_recv()
            source = at_y[8 - k][0]
            if h == step:
                y_copies.append(share(source, h, k, 8 + step))
            y_copies.append(share(source, h, near_k, 10 + 2 * h + step))
    for copy in y_copies:
        copy.wait_recv()
    c_copies = []
    masks = [recv_k[i].astype(jnp.float32) for i in range(4)]
    low_data = full[0:4].reshape(384, 256)
    high_data = full[4:8].reshape(384, 256)
    for t in range(4):
        both = dot(low_data, onehot[0, :, 256 * t : 256 * t + 256]) + dot(
            high_data, onehot[1, :, 256 * t : 256 * t + 256]
        )
        re = [[None] * 3 for _ in range(3)]
        im = [[None] * 3 for _ in range(3)]
        for w in range(8):
            row = 2 * t + w % 2
            mask = jnp.broadcast_to(masks[w // 2][row : row + 1], (8, 128))
            base = 48 * w

            def part(c, ri, side):
                at = base + 16 * c + 8 * ri
                return both[at : at + 8, 128 * side : 128 * side + 128]

            first = [(part(c, 0, 0) * mask, part(c, 1, 0) * mask) for c in range(3)]
            second = [(part(c, 0, 1), part(c, 1, 1)) for c in range(3)]
            for c in range(3):
                for d in range(3):
                    ar, ai = first[c]
                    br, bi = second[d]
                    new_re, new_im = ar * br + ai * bi, ai * br - ar * bi
                    re[c][d] = new_re if w == 0 else re[c][d] + new_re
                    im[c][d] = new_im if w == 0 else im[c][d] + new_im
        flat = []
        for i in range(3):
            for j in range(3):
                flat += [re[i][j], im[i][j]]
        main = jnp.concatenate(flat[:16], axis=0).T
        rest = jnp.concatenate(flat[16:], axis=0).T
        rest = jnp.concatenate([rest, jnp.zeros((128, 112), jnp.float32)], axis=1)
        for half_id in range(2):
            packed = jnp.zeros((8, 128), jnp.float32)
            for i in range(8):
                piece = rest[64 * half_id + 8 * i : 64 * half_id + 8 * i + 8]
                piece = pltpu.roll(piece, 16 * i, 1) if i else piece
                packed = jnp.where(lane8 // 16 == i, piece, packed)
            send_c[2 * t + half_id] = jnp.concatenate(
                [main[64 * half_id : 64 * half_id + 64], packed, jnp.zeros((8, 128), jnp.float32)], axis=0
            ).astype(jnp.bfloat16)

    for k in (4, 3, 5, 2, 6, 1, 7):
        other, target = at_x[k]
        c_copies.append(send(send_c.at[other], recv_c.at[xc], c_s.at[k], c_r.at[k], target))
    recv_c[xc] = send_c[xc]
    for copy in c_copies:
        copy.wait_recv()
    rest = swap_groups([recv_c[i, 64:80].astype(jnp.float32)[0:8] for i in range(8)], 16)
    for pair in range(4):
        pieces = [recv_c[i, 16 * pair : 16 * pair + 16].astype(jnp.float32) for i in range(8)]
        swapped = swap_groups(pieces, 16)
        for j in range(2):
            send_d[2 * pair + j] = jnp.concatenate(
                [piece[8 * j : 8 * j + 8] for piece in swapped]
                + [rest[2 * pair + j], jnp.zeros((8, 128), jnp.float32)],
                axis=0,
            ).astype(jnp.bfloat16)
    d_copies = []
    for k in (4, 3, 5, 2, 6, 1, 7):
        other, target = at_z[k]
        d_copies.append(send(send_d.at[other], recv_d.at[z], d_s.at[k], d_r.at[k], target))
    recv_d[z] = send_d[z]

    loads[7].wait()
    loads[6].wait()
    angles = jnp.concatenate([angle_ref[...], jnp.zeros((2, 120), jnp.float32)], axis=1)
    angles = jnp.concatenate([angles, jnp.zeros((6, 128), jnp.float32)], axis=0)
    sine, cosine = jnp.sin(angles).T[0:8], jnp.cos(angles).T[0:8]
    s0, s1, c0, c1 = [
        jnp.broadcast_to(value[:, i : i + 1], (8, 128)) for value in (sine, cosine) for i in range(2)
    ]
    for copy in d_copies:
        copy.wait_recv()
    ordered = []
    for block in range(8):
        got = recv_d[block].astype(jnp.float32)
        grid = [[got[24 * i + 8 * j : 24 * i + 8 * j + 8] for j in range(3)] for i in range(3)]
        for j in range(3):
            e, n = grid[0][j], grid[1][j]
            grid[0][j], grid[1][j] = s0 * e + c0 * n, s0 * n - c0 * e
        for i in range(3):
            e, n = grid[i][0], grid[i][1]
            grid[i][0], grid[i][1] = s1 * e + c1 * n, s1 * n - c1 * e
        rotated = jnp.concatenate(grid[0] + grid[1] + grid[2] + [zero8], axis=0)
        ordered.append(rotated.astype(jnp.bfloat16).astype(jnp.float32))
    left0 = jnp.concatenate(ordered[0:2], axis=1).astype(jnp.bfloat16)
    left2 = jnp.concatenate(ordered[2:4], axis=1).astype(jnp.bfloat16)
    at_re = lanes((80, 128)) // 8 % 2 == 0
    turned = []
    for t in range(4, 8):
        re_part, im_part = pltpu.roll(ordered[t], 8, 1), pltpu.roll(ordered[t], 120, 1)
        turned.append(jnp.where(at_re, -im_part, re_part) if t < 6 else jnp.where(at_re, im_part, -re_part))
    left1 = jnp.concatenate(
        [jnp.concatenate(ordered[4:8], axis=1), jnp.concatenate(turned, axis=1)], axis=0
    ).astype(jnp.bfloat16)
    scale = 1.0 / math.sqrt(NF)
    for n in range(4):
        cols = slice(256 * n, 256 * n + 256)
        e0 = dot(left0, inv[0:256, cols])
        e2 = dot(left2, inv[256:512, cols])
        odd = dot(left1, inv[512:1024, cols])
        plus, minus = e0 + e2, e0 - e2
        odd_p, odd_n = odd[0:80], odd[80:160]
        for i, value in enumerate((plus + odd_p, minus + odd_n, plus - odd_p, minus - odd_n)):
            value = (value[0:72] * scale).reshape(9, 8, 256).astype(jnp.bfloat16)
            at = QUARTER * i + 256 * n
            out_ref[:, :, at : at + 256] = value

    for copy in pending:
        copy.wait_send()


def on_device(records, station_row, pair_list, keep_mask, azimuth):
    forward, near, inverse = tables()
    own_pairs = azimuth.shape[1]
    bf16, f32 = jnp.bfloat16, jnp.float32
    dma = pltpu.SemaphoreType.DMA
    lagged = pl.pallas_call(
        kernel,
        out_shape=jax.ShapeDtypeStruct((9, own_pairs, NL), bf16),
        in_specs=[pl.BlockSpec(memory_space=pltpu.HBM)] * 8,
        out_specs=pl.BlockSpec(memory_space=pltpu.VMEM),
        scratch_shapes=[
            pltpu.VMEM(records.shape, bf16),
            pltpu.SMEM(station_row.shape, jnp.int32),
            pltpu.SMEM(pair_list.shape[::-1], jnp.int32),
            pltpu.VMEM(keep_mask.shape, jnp.int32),
            pltpu.VMEM(azimuth.shape, f32),
            pltpu.VMEM((24, NT), f32),
            pltpu.VMEM((QUARTER, 2 * NF), bf16),
            pltpu.VMEM((NF, NF), bf16),
            pltpu.VMEM((2 * NF, QUARTER), bf16),
            pltpu.VMEM((8, 32, 128), bf16),
            pltpu.VMEM((8, 32, 128), bf16),
            pltpu.VMEM((8, 16, 256), bf16),
            pltpu.VMEM((8, 16, 256), bf16),
            pltpu.VMEM((8, 96, 256), bf16),
            pltpu.VMEM((2, 256, 1024), bf16),
            pltpu.VMEM((4, 16, 128), bf16),
            pltpu.VMEM((4, 16, 128), bf16),
            pltpu.VMEM((8, 80, 128), bf16),
            pltpu.VMEM((8, 80, 128), bf16),
            pltpu.VMEM((8, 80, 128), bf16),
            pltpu.VMEM((8, 80, 128), bf16),
            dma((8,)),
        ]
        + [dma((8,))] * 4
        + [dma((14,))] * 2
        + [dma((8,))] * 6,
        compiler_params=pltpu.CompilerParams(
            collective_id=0, has_side_effects=True, vmem_limit_bytes=48 << 20
        ),
        name="correlate",
    )(
        *[
            pltpu.with_memory_space_constraint(operand, pltpu.HBM)
            for operand in (records, station_row, pair_list.T, keep_mask, azimuth, forward, near, inverse)
        ]
    )
    return jnp.transpose(lagged, (1, 0, 2))


def solution(mesh):
    in_specs = (
        P("win", None, "blk", None),
        P(),
        P("blk", None),
        P("win", "blk"),
        P(None, ("blk", "win")),
    )
    out_specs = P(("blk", "win"), None, None)
    return jax.shard_map(
        on_device, mesh=mesh, in_specs=in_specs, out_specs=out_specs, check_vma=False
    )
```

```python
import math

import jax
import jax.numpy as jnp
import numpy as np
from jax import lax
from jax.experimental import pallas as pl
from jax.experimental.pallas import tpu as pltpu
from jax.sharding import PartitionSpec as P

NT = 4096
NF = 512
FLO = 16
SMOOTH = 11
NL = 4096
QUARTER = 1024
EPSILON = 1e-05

RESIDUE = (0, 0, 2, 2, 1, 1, 3, 3)
MESH = pl.DeviceIdType.MESH


def bin_order():
    place = np.arange(64)
    return np.stack([4 * ((block % 2) * 64 + place) + RESIDUE[block] for block in range(8)])


def tables():
    bins = bin_order()
    samples = np.arange(QUARTER)

    def phase(bin_ids, times):
        return (2.0 * math.pi / NT) * ((bin_ids[..., None] + FLO) * times % NT)

    ahead = phase(bins, samples)
    forward = np.concatenate([np.cos(ahead), -np.sin(ahead)], axis=1).reshape(2 * NF, QUARTER).T
    back = phase(bins, samples - NL // 2 + NT)
    back = back.reshape(8, 8, 8, QUARTER)
    inverse = np.stack([np.cos(back), -np.sin(back)], axis=2).reshape(2 * NF, QUARTER)
    flat = bins.reshape(-1)
    apart = np.abs(flat[:, None] - flat[None, :])
    near = np.minimum(apart, NF - apart) <= SMOOTH
    return (
        jnp.asarray(forward.astype(jnp.bfloat16)),
        jnp.asarray(near.astype(jnp.bfloat16)),
        jnp.asarray(inverse.astype(jnp.bfloat16)),
    )


def dot(left, right):
    return jnp.dot(left, right, preferred_element_type=jnp.float32)


def split(value):
    lead = value.astype(jnp.bfloat16).astype(jnp.float32)
    return jnp.concatenate([lead, value - lead], axis=0).astype(jnp.bfloat16)


def lanes(shape):
    return lax.broadcasted_iota(jnp.int32, shape, len(shape) - 1)


def swap_groups(vecs, group):
    vecs = list(vecs)
    lane_group = lanes(vecs[0].shape) // group
    for step in (1, 2, 4):
        high = (lane_group // step) % 2 == 1
        for i in range(8):
            if i & step:
                continue
            low_vec, high_vec = vecs[i], vecs[i + step]
            vecs[i] = jnp.where(high, pltpu.roll(high_vec, group * step, 1), low_vec)
            vecs[i + step] = jnp.where(high, high_vec, pltpu.roll(low_vec, 128 - group * step, 1))
    return vecs


def kernel(
    rec_hbm, station_hbm, pair_hbm, keep_hbm, angle_hbm, fwd_hbm, near_hbm, inv_hbm, out_ref,
    rec_ref, station_ref, pair_ref, keep_ref, angle_ref,
    rows32, fwd, near, inv, send_a, recv_a, send_b, recv_b, full, joined, onehot,
    send_c, recv_c, send_d, recv_d,
    tab_sem, a_s, a_r, b_s, b_r, z_s, z_r, c_s, c_r, d_s, d_r,
):
    blk = lax.axis_index("blk")
    win = lax.axis_index("win")
    y_hi, x = lax.div(blk, 64), lax.rem(lax.div(blk, 16), 4)
    z, core = lax.rem(lax.div(blk, 2), 8), lax.rem(blk, 2)
    a, b = x * 2 + core, y_hi * 4 + win

    at_a, at_b, at_z = {}, {}, {}
    for k in range(1, 8):
        other = lax.rem(a + k, 8)
        at_a[k] = other, (y_hi * 64 + lax.div(other, 2) * 16 + z * 2 + lax.rem(other, 2), win)
        other = lax.rem(b + k, 8)
        at_b[k] = other, (blk + (lax.div(other, 4) - y_hi) * 64, lax.rem(other, 4))
    for k in (1, 2, 6, 7):
        other = lax.rem(z + k, 8)
        at_z[k] = other, (blk + (other - z) * 2, win)

    loads = [
        pltpu.make_async_copy(src, dst, tab_sem.at[i])
        for i, (src, dst) in enumerate(
            (
                (rec_hbm, rec_ref),
                (fwd_hbm, fwd),
                (near_hbm, near),
                (keep_hbm, keep_ref),
                (station_hbm, station_ref),
                (pair_hbm, pair_ref),
                (angle_hbm, angle_ref),
                (inv_hbm, inv),
            )
        )
    ]
    for copy in loads[:7]:
        copy.start()

    barrier = pltpu.get_barrier_semaphore()
    for at in (at_b, at_z, at_a):
        for k in at:
            pl.semaphore_signal(barrier, inc=1, device_id=at[k][1], device_id_type=MESH)

    pending = []

    def send(src, dst, sem_s, sem_r, target):
        copy = pltpu.make_async_remote_copy(
            src_ref=src, dst_ref=dst, send_sem=sem_s, recv_sem=sem_r, device_id=target, device_id_type=MESH
        )
        copy.start()
        pending.append(copy)
        return copy

    for copy in loads[3:6]:
        copy.wait()
    lane8, lane16 = lanes((8, 128)), lanes((16, 128))
    row8 = lax.broadcasted_iota(jnp.int32, (8, 128), 0)
    zero8 = jnp.zeros((8, 128), jnp.float32)
    record = jnp.zeros((8, 128), jnp.int32)
    for p in range(8):
        for side in range(2):
            spot = jnp.logical_and(row8 == side, lane8 == p)
            record = jnp.where(spot, station_ref[pair_ref[side, win * 8 + p]], record)
    r_hi, r_x, r_z = record // 256, record // 64 % 4, record // 8 % 8
    r_c, r_s = record // 4 % 2, record % 4
    place = r_z * 64 + r_hi * 32 + (r_x * 2 + r_c) * 4 + r_s
    first_digit = (place // 16).astype(jnp.float32)
    second_digit = (place % 16).astype(jnp.float32)
    keep = jnp.concatenate([keep_ref[...].astype(jnp.float32), jnp.zeros((2, 96), jnp.float32)], axis=1)
    keep = jnp.concatenate([keep, jnp.zeros((6, 128), jnp.float32)], axis=0)
    digits = jnp.where(row8 < 6, pltpu.roll(first_digit, 4, 0), pltpu.roll(second_digit, 6, 0))
    own_table = (digits, pltpu.roll(keep, 4, 0))

    loads[0].wait()
    for w in range(2):
        for c in range(3):
            rows32[c * 8 + w * 4 : c * 8 + w * 4 + 4, :] = rec_ref[w, c].astype(jnp.float32)
    q0, q1, q2, q3 = [rows32[:, QUARTER * i : QUARTER * (i + 1)] for i in range(4)]
    s02, s13, d02, d13 = q0 + q2, q1 + q3, q0 - q2, q1 - q3
    left0, left2 = split(s02 + s13), split(s02 - s13)
    left1 = jnp.concatenate([split(d02), split(d13)], axis=0)

    loads[1].wait()
    got0 = dot(left0, fwd[:, 0:256])
    got2 = dot(left2, fwd[:, 256:512])
    got1 = dot(left1, fwd[:, 512:1024])
    even = jnp.concatenate([got0[:24] + got0[24:], got2[:24] + got2[24:]], axis=1)
    odd_a = got1[0:24] + got1[24:48]
    odd_b = got1[48:72] + got1[72:96]
    half = lanes((24, 128)) < 64
    spec = [even[:, 128 * t : 128 * t + 128] for t in range(4)]
    for t in range(4):
        turned = pltpu.roll(odd_b[:, 128 * t : 128 * t + 128], 64, 1)
        plus = half if t < 2 else jnp.logical_not(half)
        spec.append(odd_a[:, 128 * t : 128 * t + 128] + jnp.where(plus, turned, -turned))
    spec = [piece * (1.0 / math.sqrt(NT)) for piece in spec]

    low_half = row8 < 4
    half8 = lanes((8, 128)) < 64
    energy = []
    for piece in spec:
        square = piece * piece
        total = square[0:8] + square[8:16] + square[16:24]
        energy.append(total + pltpu.roll(total, 64, 1))
    energy = jnp.concatenate([jnp.where(half8, energy[2 * j], energy[2 * j + 1]) for j in range(4)], axis=1)
    loads[2].wait()
    smooth = dot(split(energy), near[...])
    smooth = smooth[0:8] + smooth[8:16]
    amp = lax.rsqrt(smooth / (3.0 * (2 * SMOOTH + 1)) + EPSILON)
    for t in range(8):
        piece = amp[:, 128 * (t // 2) : 128 * (t // 2) + 128]
        turned = pltpu.roll(piece, 64, 1)
        wide = jnp.where(half8, piece, turned) if t % 2 == 0 else jnp.where(half8, turned, piece)
        white = [spec[t][8 * c : 8 * c + 8] * wide for c in range(3)]
        for w in range(2):
            v0, v1, v2 = white if w == 0 else [pltpu.roll(value, 4, 0) for value in white]
            v1 = pltpu.roll(v1, 4, 0)
            chunk = [jnp.where(low_half, v0, v1), jnp.where(low_half, v2, own_table[w])]
            send_a[w, t] = jnp.concatenate(chunk, axis=0).astype(jnp.bfloat16)

    pl.semaphore_wait(barrier, 18)

    far_first = (4, 3, 5, 2, 6, 1, 7)
    a_copies = [[], []]
    for w in range(2):
        for k in far_first:
            other, target = at_a[k]
            a_copies[w].append(
                send(send_a.at[w, other], recv_a.at[w, a], a_s.at[8 * w + k], a_r.at[8 * w + k], target)
            )
        recv_a[w, a] = send_a[w, a]
    loads[7].start()

    b_copies = [[], []]
    for w in range(2):
        for copy in a_copies[w]:
            copy.wait_recv()
        got = [recv_a[w, i].astype(jnp.float32) for i in range(8)]
        tops, lows = [value[0:8] for value in got], [value[8:16] for value in got]
        stacked = []
        for c in range(3):
            parts = tops if c < 2 else lows
            for j in range(4):
                first, second = parts[2 * j], parts[2 * j + 1]
                if c == 1:
                    stacked.append(jnp.where(low_half, pltpu.roll(first, 4, 0), second))
                else:
                    stacked.append(jnp.where(low_half, first, pltpu.roll(second, 4, 0)))
        stacked += [zero8] * 4
        turn = jnp.concatenate(stacked, axis=0).T

        def spread(a_half, q):
            merged = zero8
            for i in range(4):
                piece = pltpu.roll(lows[4 * a_half + i], (96 + 8 * i - 8 * q) % 128, 1)
                merged = jnp.where(lane8 // 8 == 12 + i, piece, merged)
            return merged

        if w == 0:
            tail = [jnp.where(low_half, pltpu.roll(spread(0, 0), 4, 0), spread(1, 0)), zero8]
        else:
            tail = []
            for a_half in range(2):
                merged = zero8
                for q in range(4):
                    piece = spread(a_half, q)
                    piece = piece if q == 2 else pltpu.roll(piece, (2 * q + 4) % 8, 0)
                    merged = jnp.where(row8 // 2 == q, piece, merged)
                tail.append(merged)
        for i in range(8):
            send_b[w, i] = jnp.concatenate(
                [turn[8 * i : 8 * i + 8] + tail[0], turn[64 + 8 * i : 72 + 8 * i] + tail[1]], axis=0
            ).astype(jnp.bfloat16)
        for k in far_first:
            other, target = at_b[k]
            b_copies[w].append(
                send(send_b.at[w, other], recv_b.at[w, b], b_s.at[8 * w + k], b_r.at[8 * w + k], target)
            )
        recv_b[w, b] = send_b[w, b]

    def share(source, h, k, sem):
        block = full.at[source, pl.ds(96 * h, 96)]
        return send(block, block, z_s.at[sem], z_r.at[sem], at_z[k][1])

    direct = {}
    tables_got = []
    for w in range(2):
        for copy in b_copies[w]:
            copy.wait_recv()
        got = [recv_b[w, i].astype(jnp.float32) for i in range(8)]
        mine = []
        for odd in range(2):
            for c in range(3):
                out = None
                for j in range(4):
                    piece = got[4 * (j % 2) + 2 * (j // 2) + odd]
                    shift = (32 * (j - c)) % 128
                    piece = pltpu.roll(piece, shift, 1) if shift else piece
                    out = piece if out is None else jnp.where(lane16 // 32 == j, piece, out)
                mine.append(out)
        full[z, 96 * w : 96 * w + 96] = jnp.concatenate(mine, axis=0).astype(jnp.bfloat16)
        for k in (2, 6):
            direct[k, w] = share(z, w, k, len(direct))
        table = []
        for t in range(4):
            merged = zero8
            for j in range(4):
                shift = (32 + 32 * j) % 128
                here = lane8 // 32 == j
                if w == 0:
                    piece = got[2 * t + j // 2][0:8]
                    piece = pltpu.roll(piece, 4, 0) if j % 2 else piece
                    piece = pltpu.roll(piece, shift, 1) if shift else piece
                    merged = jnp.where(here, piece, merged)
                    continue
                for q in range(4):
                    piece = got[4 * (t // 2) + q][8 * (j % 2) : 8 * (j % 2) + 8]
                    down = (2 * q - 2 * (2 * t % 4 + j // 2)) % 8
                    piece = pltpu.roll(piece, down, 0) if down else piece
                    piece = pltpu.roll(piece, shift, 1) if shift else piece
                    merged = jnp.where(jnp.logical_and(here, row8 // 2 == q), piece, merged)
            table.append(merged)
        tables_got.append(table)
    z_copies = []
    for w in range(2):
        for k in (1, 7):
            direct[k, w] = share(z, w, k, len(direct))
            z_copies.append(direct[k, w])
    info, keeps = tables_got

    place_ids = lax.broadcasted_iota(jnp.int32, (512, 128), 0)
    for t in range(4):
        for side in range(2):
            place = (16.0 * info[t][side : side + 1] + info[t][2 + side : 3 + side]).astype(jnp.int32)
            at = 256 * t + 128 * side
            onehot[:, at : at + 128] = jnp.where(place_ids == place, 1.0, 0.0).astype(jnp.bfloat16)

    for h in range(2):
        for step, (k, near_k) in enumerate(((2, 1), (6, 7))):
            direct[k, h].wait_recv()
            source = at_z[8 - k][0]
            if h == step:
                z_copies.append(share(source, h, k, 8 + step))
            z_copies.append(share(source, h, near_k, 10 + 2 * h + step))
    for copy in z_copies:
        copy.wait_recv()
    c_copies = []
    low_lanes = lanes((192, 128)) < 64
    for j in range(4):
        first, second = full[2 * j].astype(jnp.float32), full[2 * j + 1].astype(jnp.float32)
        cols = slice(128 * j, 128 * j + 128)
        joined[0, :, cols] = jnp.where(low_lanes, first, pltpu.roll(second, 64, 1)).astype(jnp.bfloat16)
        joined[1, :, cols] = jnp.where(low_lanes, pltpu.roll(first, 64, 1), second).astype(jnp.bfloat16)
    for t in range(4):
        halves = [dot(joined[i], onehot[:, 256 * t : 256 * t + 256]) for i in range(2)]
        re = [[None] * 3 for _ in range(3)]
        im = [[None] * 3 for _ in range(3)]
        for w in range(8):
            mask = jnp.broadcast_to(keeps[t][w : w + 1], (8, 128))
            both = halves[w // 4]
            base = 96 * (w % 2) + 48 * (w // 2 % 2)

            def part(c, ri, side):
                at = base + 16 * c + 8 * ri
                return both[at : at + 8, 128 * side : 128 * side + 128]

            first = [(part(c, 0, 0) * mask, part(c, 1, 0) * mask) for c in range(3)]
            second = [(part(c, 0, 1), part(c, 1, 1)) for c in range(3)]
            for c in range(3):
                for d in range(3):
                    ar, ai = first[c]
                    br, bi = second[d]
                    new_re, new_im = ar * br + ai * bi, ai * br - ar * bi
                    re[c][d] = new_re if w == 0 else re[c][d] + new_re
                    im[c][d] = new_im if w == 0 else im[c][d] + new_im
        flat = []
        for i in range(3):
            for j in range(3):
                flat += [re[i][j], im[i][j]]
        main = jnp.concatenate(flat[:16], axis=0).T
        rest = jnp.concatenate(flat[16:], axis=0).T
        rest = jnp.concatenate([rest, jnp.zeros((128, 112), jnp.float32)], axis=1)
        for half_id in range(2):
            packed = jnp.zeros((8, 128), jnp.float32)
            for i in range(8):
                piece = rest[64 * half_id + 8 * i : 64 * half_id + 8 * i + 8]
                piece = pltpu.roll(piece, 16 * i, 1) if i else piece
                packed = jnp.where(lane8 // 16 == i, piece, packed)
            send_c[2 * t + half_id] = jnp.concatenate(
                [main[64 * half_id : 64 * half_id + 64], packed, jnp.zeros((8, 128), jnp.float32)], axis=0
            ).astype(jnp.bfloat16)

    for k in (4, 3, 5, 2, 6, 1, 7):
        other, target = at_b[k]
        c_copies.append(send(send_c.at[other], recv_c.at[b], c_s.at[k], c_r.at[k], target))
    recv_c[b] = send_c[b]
    for copy in c_copies:
        copy.wait_recv()
    rest = swap_groups([recv_c[i, 64:80].astype(jnp.float32)[0:8] for i in range(8)], 16)
    for pair in range(4):
        pieces = [recv_c[i, 16 * pair : 16 * pair + 16].astype(jnp.float32) for i in range(8)]
        swapped = swap_groups(pieces, 16)
        for j in range(2):
            send_d[2 * pair + j] = jnp.concatenate(
                [piece[8 * j : 8 * j + 8] for piece in swapped]
                + [rest[2 * pair + j], jnp.zeros((8, 128), jnp.float32)],
                axis=0,
            ).astype(jnp.bfloat16)
    d_copies = []
    for k in (4, 3, 5, 2, 6, 1, 7):
        other, target = at_a[k]
        d_copies.append(send(send_d.at[other], recv_d.at[a], d_s.at[k], d_r.at[k], target))
    recv_d[a] = send_d[a]

    loads[7].wait()
    loads[6].wait()
    angles = jnp.concatenate([angle_ref[...], jnp.zeros((2, 120), jnp.float32)], axis=1)
    angles = jnp.concatenate([angles, jnp.zeros((6, 128), jnp.float32)], axis=0)
    sine, cosine = jnp.sin(angles).T[0:8], jnp.cos(angles).T[0:8]
    s0, s1, c0, c1 = [
        jnp.broadcast_to(value[:, i : i + 1], (8, 128)) for value in (sine, cosine) for i in range(2)
    ]
    for copy in d_copies:
        copy.wait_recv()
    ordered = []
    for block in range(8):
        got = recv_d[block].astype(jnp.float32)
        grid = [[got[24 * i + 8 * j : 24 * i + 8 * j + 8] for j in range(3)] for i in range(3)]
        for j in range(3):
            e, n = grid[0][j], grid[1][j]
            grid[0][j], grid[1][j] = s0 * e + c0 * n, s0 * n - c0 * e
        for i in range(3):
            e, n = grid[i][0], grid[i][1]
            grid[i][0], grid[i][1] = s1 * e + c1 * n, s1 * n - c1 * e
        rotated = jnp.concatenate(grid[0] + grid[1] + grid[2] + [zero8], axis=0)
        ordered.append(rotated.astype(jnp.bfloat16).astype(jnp.float32))
    left0 = jnp.concatenate(ordered[0:2], axis=1).astype(jnp.bfloat16)
    left2 = jnp.concatenate(ordered[2:4], axis=1).astype(jnp.bfloat16)
    at_re = lanes((80, 128)) // 8 % 2 == 0
    turned = []
    for t in range(4, 8):
        re_part, im_part = pltpu.roll(ordered[t], 8, 1), pltpu.roll(ordered[t], 120, 1)
        turned.append(jnp.where(at_re, -im_part, re_part) if t < 6 else jnp.where(at_re, im_part, -re_part))
    left1 = jnp.concatenate(
        [jnp.concatenate(ordered[4:8], axis=1), jnp.concatenate(turned, axis=1)], axis=0
    ).astype(jnp.bfloat16)
    scale = 1.0 / math.sqrt(NF)
    for n in range(4):
        cols = slice(256 * n, 256 * n + 256)
        e0 = dot(left0, inv[0:256, cols])
        e2 = dot(left2, inv[256:512, cols])
        odd = dot(left1, inv[512:1024, cols])
        plus, minus = e0 + e2, e0 - e2
        odd_p, odd_n = odd[0:80], odd[80:160]
        for i, value in enumerate((plus + odd_p, minus + odd_n, plus - odd_p, minus - odd_n)):
            value = (value[0:72] * scale).reshape(9, 8, 256).astype(jnp.bfloat16)
            at = QUARTER * i + 256 * n
            out_ref[:, :, at : at + 256] = value

    for copy in pending:
        copy.wait_send()


def on_device(records, station_row, pair_list, keep_mask, azimuth):
    forward, near, inverse = tables()
    own_pairs = azimuth.shape[1]
    bf16, f32 = jnp.bfloat16, jnp.float32
    dma = pltpu.SemaphoreType.DMA
    lagged = pl.pallas_call(
        kernel,
        out_shape=jax.ShapeDtypeStruct((9, own_pairs, NL), bf16),
        in_specs=[pl.BlockSpec(memory_space=pltpu.HBM)] * 8,
        out_specs=pl.BlockSpec(memory_space=pltpu.VMEM),
        scratch_shapes=[
            pltpu.VMEM(records.shape, bf16),
            pltpu.SMEM(station_row.shape, jnp.int32),
            pltpu.SMEM(pair_list.shape[::-1], jnp.int32),
            pltpu.VMEM(keep_mask.shape, jnp.int32),
            pltpu.VMEM(azimuth.shape, f32),
            pltpu.VMEM((24, NT), f32),
            pltpu.VMEM((QUARTER, 2 * NF), bf16),
            pltpu.VMEM((NF, NF), bf16),
            pltpu.VMEM((2 * NF, QUARTER), bf16),
            pltpu.VMEM((2, 8, 16, 128), bf16),
            pltpu.VMEM((2, 8, 16, 128), bf16),
            pltpu.VMEM((2, 8, 16, 128), bf16),
            pltpu.VMEM((2, 8, 16, 128), bf16),
            pltpu.VMEM((8, 192, 128), bf16),
            pltpu.VMEM((2, 192, 512), bf16),
            pltpu.VMEM((512, 1024), bf16),
            pltpu.VMEM((8, 80, 128), bf16),
            pltpu.VMEM((8, 80, 128), bf16),
            pltpu.VMEM((8, 80, 128), bf16),
            pltpu.VMEM((8, 80, 128), bf16),
            dma((8,)),
        ]
        + [dma((16,))] * 4
        + [dma((14,))] * 2
        + [dma((8,))] * 4,
        compiler_params=pltpu.CompilerParams(
            collective_id=0, has_side_effects=True, vmem_limit_bytes=48 << 20
        ),
        name="correlate",
    )(
        *[
            pltpu.with_memory_space_constraint(operand, pltpu.HBM)
            for operand in (records, station_row, pair_list.T, keep_mask, azimuth, forward, near, inverse)
        ]
    )
    return jnp.transpose(lagged, (1, 0, 2))


def solution(mesh):
    in_specs = (
        P("win", None, "blk", None),
        P(),
        P("blk", None),
        P("win", "blk"),
        P(None, ("blk", "win")),
    )
    out_specs = P(("blk", "win"), None, None)
    return jax.shard_map(
        on_device, mesh=mesh, in_specs=in_specs, out_specs=out_specs, check_vma=False
    )
```

```python
import math

import jax
import jax.numpy as jnp
import numpy as np
from jax import lax
from jax.experimental import pallas as pl
from jax.experimental.pallas import tpu as pltpu
from jax.sharding import PartitionSpec as P

NT = 4096
NF = 512
FLO = 16
SMOOTH = 11
NL = 4096
QUARTER = 1024
EPSILON = 1e-05

RESIDUE = (0, 0, 2, 2, 1, 1, 3, 3)
MESH = pl.DeviceIdType.MESH


def bin_order():
    place = np.arange(64)
    return np.stack([4 * ((block % 2) * 64 + place) + RESIDUE[block] for block in range(8)])


def tables():
    bins = bin_order()
    samples = np.arange(QUARTER)

    def phase(bin_ids, times):
        return (2.0 * math.pi / NT) * ((bin_ids[..., None] + FLO) * times % NT)

    ahead = phase(bins, samples)
    forward = np.concatenate([np.cos(ahead), -np.sin(ahead)], axis=1).reshape(2 * NF, QUARTER).T
    back = phase(bins, samples - NL // 2 + NT)
    back = back.reshape(8, 8, 8, QUARTER)
    inverse = np.stack([np.cos(back), -np.sin(back)], axis=2).reshape(2 * NF, QUARTER)
    flat = bins.reshape(-1)
    apart = np.abs(flat[:, None] - flat[None, :])
    near = np.minimum(apart, NF - apart) <= SMOOTH
    return (
        jnp.asarray(forward.astype(jnp.bfloat16)),
        jnp.asarray(near.astype(jnp.bfloat16)),
        jnp.asarray(inverse.astype(jnp.bfloat16)),
    )


def dot(left, right):
    return jnp.dot(left, right, preferred_element_type=jnp.float32)


def split(value):
    lead = value.astype(jnp.bfloat16).astype(jnp.float32)
    return jnp.concatenate([lead, value - lead], axis=0).astype(jnp.bfloat16)


def lanes(shape):
    return lax.broadcasted_iota(jnp.int32, shape, len(shape) - 1)


def swap_groups(vecs, group):
    vecs = list(vecs)
    lane_group = lanes(vecs[0].shape) // group
    for step in (1, 2, 4):
        high = (lane_group // step) % 2 == 1
        for i in range(8):
            if i & step:
                continue
            low_vec, high_vec = vecs[i], vecs[i + step]
            vecs[i] = jnp.where(high, pltpu.roll(high_vec, group * step, 1), low_vec)
            vecs[i + step] = jnp.where(high, high_vec, pltpu.roll(low_vec, 128 - group * step, 1))
    return vecs


def kernel(
    rec_hbm, station_hbm, pair_hbm, keep_hbm, angle_hbm, fwd_hbm, near_hbm, inv_hbm, out_ref,
    rec_ref, station_ref, pair_ref, keep_ref, angle_ref,
    rows32, fwd, near, inv, send_a, recv_a, send_b, recv_b, full, joined, onehot,
    send_c, recv_c, send_d, recv_d,
    tab_sem, a_s, a_r, b_s, b_r, z_s, z_r, c_s, c_r, d_s, d_r,
):
    blk = lax.axis_index("blk")
    win = lax.axis_index("win")
    y_hi, x = lax.div(blk, 64), lax.rem(lax.div(blk, 16), 4)
    z, core = lax.rem(lax.div(blk, 2), 8), lax.rem(blk, 2)
    a, b = x * 2 + core, y_hi * 4 + win

    at_a, at_b, at_z = {}, {}, {}
    for k in range(1, 8):
        other = lax.rem(a + k, 8)
        at_a[k] = other, (y_hi * 64 + lax.div(other, 2) * 16 + z * 2 + lax.rem(other, 2), win)
        other = lax.rem(b + k, 8)
        at_b[k] = other, (blk + (lax.div(other, 4) - y_hi) * 64, lax.rem(other, 4))
    for k in (1, 2, 6, 7):
        other = lax.rem(z + k, 8)
        at_z[k] = other, (blk + (other - z) * 2, win)

    loads = [
        pltpu.make_async_copy(src, dst, tab_sem.at[i])
        for i, (src, dst) in enumerate(
            (
                (rec_hbm, rec_ref),
                (fwd_hbm, fwd),
                (near_hbm, near),
                (keep_hbm, keep_ref),
                (station_hbm, station_ref),
                (pair_hbm, pair_ref),
                (angle_hbm, angle_ref),
                (inv_hbm, inv),
            )
        )
    ]
    for copy in loads[:7]:
        copy.start()

    barrier = pltpu.get_barrier_semaphore()
    for at in (at_b, at_z, at_a):
        for k in at:
            pl.semaphore_signal(barrier, inc=1, device_id=at[k][1], device_id_type=MESH)

    pending = []

    def send(src, dst, sem_s, sem_r, target):
        copy = pltpu.make_async_remote_copy(
            src_ref=src, dst_ref=dst, send_sem=sem_s, recv_sem=sem_r, device_id=target, device_id_type=MESH
        )
        copy.start()
        pending.append(copy)
        return copy

    for copy in loads[3:6]:
        copy.wait()
    lane8, lane16 = lanes((8, 128)), lanes((16, 128))
    row8 = lax.broadcasted_iota(jnp.int32, (8, 128), 0)
    zero8 = jnp.zeros((8, 128), jnp.float32)
    record = jnp.zeros((8, 128), jnp.int32)
    for p in range(8):
        for side in range(2):
            spot = jnp.logical_and(row8 == side, lane8 == p)
            record = jnp.where(spot, station_ref[pair_ref[side, win * 8 + p]], record)
    r_hi, r_x, r_z = record // 256, record // 64 % 4, record // 8 % 8
    r_c, r_s = record // 4 % 2, record % 4
    place = r_z * 64 + r_hi * 32 + (r_x * 2 + r_c) * 4 + r_s
    first_digit = (place // 16).astype(jnp.float32)
    second_digit = (place % 16).astype(jnp.float32)
    keep = jnp.concatenate([keep_ref[...].astype(jnp.float32), jnp.zeros((2, 96), jnp.float32)], axis=1)
    keep = jnp.concatenate([keep, jnp.zeros((6, 128), jnp.float32)], axis=0)
    digits = jnp.where(row8 < 6, pltpu.roll(first_digit, 4, 0), pltpu.roll(second_digit, 6, 0))
    own_table = (digits, pltpu.roll(keep, 4, 0))

    loads[0].wait()
    for w in range(2):
        for c in range(3):
            rows32[c * 8 + w * 4 : c * 8 + w * 4 + 4, :] = rec_ref[w, c].astype(jnp.float32)
    q0, q1, q2, q3 = [rows32[:, QUARTER * i : QUARTER * (i + 1)] for i in range(4)]
    s02, s13, d02, d13 = q0 + q2, q1 + q3, q0 - q2, q1 - q3
    left0, left2 = split(s02 + s13), split(s02 - s13)
    left1 = jnp.concatenate([split(d02), split(d13)], axis=0)

    loads[1].wait()
    got0 = dot(left0, fwd[:, 0:256])
    got2 = dot(left2, fwd[:, 256:512])
    got1 = dot(left1, fwd[:, 512:1024])
    even = jnp.concatenate([got0[:24] + got0[24:], got2[:24] + got2[24:]], axis=1)
    odd_a = got1[0:24] + got1[24:48]
    odd_b = got1[48:72] + got1[72:96]
    half = lanes((24, 128)) < 64
    spec = [even[:, 128 * t : 128 * t + 128] for t in range(4)]
    for t in range(4):
        turned = pltpu.roll(odd_b[:, 128 * t : 128 * t + 128], 64, 1)
        plus = half if t < 2 else jnp.logical_not(half)
        spec.append(odd_a[:, 128 * t : 128 * t + 128] + jnp.where(plus, turned, -turned))
    spec = [piece * (1.0 / math.sqrt(NT)) for piece in spec]

    low_half = row8 < 4
    half8 = lanes((8, 128)) < 64
    energy = []
    for piece in spec:
        square = piece * piece
        total = square[0:8] + square[8:16] + square[16:24]
        energy.append(total + pltpu.roll(total, 64, 1))
    energy = jnp.concatenate([jnp.where(half8, energy[2 * j], energy[2 * j + 1]) for j in range(4)], axis=1)
    loads[2].wait()
    smooth = dot(split(energy), near[...])
    smooth = smooth[0:8] + smooth[8:16]
    amp = lax.rsqrt(smooth / (3.0 * (2 * SMOOTH + 1)) + EPSILON)
    for t in range(8):
        piece = amp[:, 128 * (t // 2) : 128 * (t // 2) + 128]
        turned = pltpu.roll(piece, 64, 1)
        wide = jnp.where(half8, piece, turned) if t % 2 == 0 else jnp.where(half8, turned, piece)
        white = [spec[t][8 * c : 8 * c + 8] * wide for c in range(3)]
        for w in range(2):
            v0, v1, v2 = white if w == 0 else [pltpu.roll(value, 4, 0) for value in white]
            v1 = pltpu.roll(v1, 4, 0)
            chunk = [jnp.where(low_half, v0, v1), jnp.where(low_half, v2, own_table[w])]
            send_a[w, t] = jnp.concatenate(chunk, axis=0).astype(jnp.bfloat16)

    pl.semaphore_wait(barrier, 18)

    far_first = (4, 3, 5, 2, 6, 1, 7)
    a_copies = [[], []]
    for w in range(2):
        for k in far_first:
            other, target = at_a[k]
            a_copies[w].append(
                send(send_a.at[w, other], recv_a.at[w, a], a_s.at[8 * w + k], a_r.at[8 * w + k], target)
            )
        recv_a[w, a] = send_a[w, a]
    loads[7].start()

    b_copies = [[], []]
    for w in range(2):
        for copy in a_copies[w]:
            copy.wait_recv()
        got = [recv_a[w, i].astype(jnp.float32) for i in range(8)]
        tops, lows = [value[0:8] for value in got], [value[8:16] for value in got]
        stacked = []
        for c in range(3):
            parts = tops if c < 2 else lows
            for j in range(4):
                first, second = parts[2 * j], parts[2 * j + 1]
                if c == 1:
                    stacked.append(jnp.where(low_half, pltpu.roll(first, 4, 0), second))
                else:
                    stacked.append(jnp.where(low_half, first, pltpu.roll(second, 4, 0)))
        stacked += [zero8] * 4
        turn = jnp.concatenate(stacked, axis=0).T

        def spread(a_half, q):
            merged = zero8
            for i in range(4):
                piece = pltpu.roll(lows[4 * a_half + i], (96 + 8 * i - 8 * q) % 128, 1)
                merged = jnp.where(lane8 // 8 == 12 + i, piece, merged)
            return merged

        if w == 0:
            tail = [jnp.where(low_half, pltpu.roll(spread(0, 0), 4, 0), spread(1, 0)), zero8]
        else:
            tail = []
            for a_half in range(2):
                merged = zero8
                for q in range(4):
                    piece = spread(a_half, q)
                    piece = piece if q == 2 else pltpu.roll(piece, (2 * q + 4) % 8, 0)
                    merged = jnp.where(row8 // 2 == q, piece, merged)
                tail.append(merged)
        for i in range(8):
            send_b[w, i] = jnp.concatenate(
                [turn[8 * i : 8 * i + 8] + tail[0], turn[64 + 8 * i : 72 + 8 * i] + tail[1]], axis=0
            ).astype(jnp.bfloat16)
        for k in far_first:
            other, target = at_b[k]
            b_copies[w].append(
                send(send_b.at[w, other], recv_b.at[w, b], b_s.at[8 * w + k], b_r.at[8 * w + k], target)
            )
        recv_b[w, b] = send_b[w, b]

    def share(source, h, k, sem):
        block = full.at[source, pl.ds(96 * h, 96)]
        return send(block, block, z_s.at[sem], z_r.at[sem], at_z[k][1])

    direct = {}
    tables_got = []
    for w in range(2):
        for copy in b_copies[w]:
            copy.wait_recv()
        got = [recv_b[w, i].astype(jnp.float32) for i in range(8)]
        mine = []
        for odd in range(2):
            for c in range(3):
                out = None
                for j in range(4):
                    piece = got[4 * (j % 2) + 2 * (j // 2) + odd]
                    shift = (32 * (j - c)) % 128
                    piece = pltpu.roll(piece, shift, 1) if shift else piece
                    out = piece if out is None else jnp.where(lane16 // 32 == j, piece, out)
                mine.append(out)
        full[z, 96 * w : 96 * w + 96] = jnp.concatenate(mine, axis=0).astype(jnp.bfloat16)
        for k in (2, 6):
            direct[k, w] = share(z, w, k, len(direct))
        table = []
        for t in range(4):
            merged = zero8
            for j in range(4):
                shift = (32 + 32 * j) % 128
                here = lane8 // 32 == j
                if w == 0:
                    piece = got[2 * t + j // 2][0:8]
                    piece = pltpu.roll(piece, 4, 0) if j % 2 else piece
                    piece = pltpu.roll(piece, shift, 1) if shift else piece
                    merged = jnp.where(here, piece, merged)
                    continue
                for q in range(4):
                    piece = got[4 * (t // 2) + q][8 * (j % 2) : 8 * (j % 2) + 8]
                    down = (2 * q - 2 * (2 * t % 4 + j // 2)) % 8
                    piece = pltpu.roll(piece, down, 0) if down else piece
                    piece = pltpu.roll(piece, shift, 1) if shift else piece
                    merged = jnp.where(jnp.logical_and(here, row8 // 2 == q), piece, merged)
            table.append(merged)
        tables_got.append(table)
    z_copies = []
    for w in range(2):
        for k in (1, 7):
            direct[k, w] = share(z, w, k, len(direct))
            z_copies.append(direct[k, w])
    info, keeps = tables_got

    place_ids = lax.broadcasted_iota(jnp.int32, (512, 128), 0)
    for t in range(4):
        for side in range(2):
            place = (16.0 * info[t][side : side + 1] + info[t][2 + side : 3 + side]).astype(jnp.int32)
            at = 256 * t + 128 * side
            onehot[:, at : at + 128] = jnp.where(place_ids == place, 1.0, 0.0).astype(jnp.bfloat16)

    for h in range(2):
        for step, (k, near_k) in enumerate(((2, 1), (6, 7))):
            direct[k, h].wait_recv()
            source = at_z[8 - k][0]
            if h == step:
                z_copies.append(share(source, h, k, 8 + step))
            z_copies.append(share(source, h, near_k, 10 + 2 * h + step))
    for copy in z_copies:
        copy.wait_recv()

    def to_owner(i):
        return pltpu.make_async_remote_copy(
            src_ref=send_c.at[i],
            dst_ref=recv_c.at[b],
            send_sem=c_s.at[i],
            recv_sem=c_r.at[b],
            device_id=(blk + (i // 4 - y_hi) * 64, i % 4),
            device_id_type=MESH,
        )

    def from_source(i):
        return pltpu.make_async_remote_copy(
            src_ref=send_c.at[i],
            dst_ref=recv_c.at[i],
            send_sem=c_s.at[i],
            recv_sem=c_r.at[i],
            device_id=(blk + (i // 4 - y_hi) * 64, i % 4),
            device_id_type=MESH,
        )

    low_lanes = lanes((192, 128)) < 64
    for j in range(4):
        first, second = full[2 * j].astype(jnp.float32), full[2 * j + 1].astype(jnp.float32)
        cols = slice(128 * j, 128 * j + 128)
        joined[0, :, cols] = jnp.where(low_lanes, first, pltpu.roll(second, 64, 1)).astype(jnp.bfloat16)
        joined[1, :, cols] = jnp.where(low_lanes, pltpu.roll(first, 64, 1), second).astype(jnp.bfloat16)
    for t in range(4):
        halves = [dot(joined[i], onehot[:, 256 * t : 256 * t + 256]) for i in range(2)]
        re = [[None] * 3 for _ in range(3)]
        im = [[None] * 3 for _ in range(3)]
        for w in range(8):
            mask = jnp.broadcast_to(keeps[t][w : w + 1], (8, 128))
            both = halves[w // 4]
            base = 96 * (w % 2) + 48 * (w // 2 % 2)

            def part(c, ri, side):
                at = base + 16 * c + 8 * ri
                return both[at : at + 8, 128 * side : 128 * side + 128]

            first = [(part(c, 0, 0) * mask, part(c, 1, 0) * mask) for c in range(3)]
            second = [(part(c, 0, 1), part(c, 1, 1)) for c in range(3)]
            for c in range(3):
                for d in range(3):
                    ar, ai = first[c]
                    br, bi = second[d]
                    new_re, new_im = ar * br + ai * bi, ai * br - ar * bi
                    re[c][d] = new_re if w == 0 else re[c][d] + new_re
                    im[c][d] = new_im if w == 0 else im[c][d] + new_im
        flat = []
        for i in range(3):
            for j in range(3):
                flat += [re[i][j], im[i][j]]
        main = jnp.concatenate(flat[:16], axis=0).T
        rest = jnp.concatenate(flat[16:], axis=0).T
        rest = jnp.concatenate([rest, jnp.zeros((128, 112), jnp.float32)], axis=1)
        for half_id in range(2):
            packed = jnp.zeros((8, 128), jnp.float32)
            for i in range(8):
                piece = rest[64 * half_id + 8 * i : 64 * half_id + 8 * i + 8]
                piece = pltpu.roll(piece, 16 * i, 1) if i else piece
                packed = jnp.where(lane8 // 16 == i, piece, packed)
            send_c[2 * t + half_id] = jnp.concatenate(
                [main[64 * half_id : 64 * half_id + 64], packed, jnp.zeros((8, 128), jnp.float32)], axis=0
            ).astype(jnp.bfloat16)
            pl.when(b != 2 * t + half_id)(to_owner(2 * t + half_id).start)

    recv_c[b] = send_c[b]
    for i in range(8):
        pl.when(b != i)(from_source(i).wait_recv)
    rest = swap_groups([recv_c[i, 64:80].astype(jnp.float32)[0:8] for i in range(8)], 16)
    for pair in range(4):
        pieces = [recv_c[i, 16 * pair : 16 * pair + 16].astype(jnp.float32) for i in range(8)]
        swapped = swap_groups(pieces, 16)
        for j in range(2):
            send_d[2 * pair + j] = jnp.concatenate(
                [piece[8 * j : 8 * j + 8] for piece in swapped]
                + [rest[2 * pair + j], jnp.zeros((8, 128), jnp.float32)],
                axis=0,
            ).astype(jnp.bfloat16)
    d_copies = []
    for k in (4, 3, 5, 2, 6, 1, 7):
        other, target = at_a[k]
        d_copies.append(send(send_d.at[other], recv_d.at[a], d_s.at[k], d_r.at[k], target))
    recv_d[a] = send_d[a]

    loads[7].wait()
    loads[6].wait()
    angles = jnp.concatenate([angle_ref[...], jnp.zeros((2, 120), jnp.float32)], axis=1)
    angles = jnp.concatenate([angles, jnp.zeros((6, 128), jnp.float32)], axis=0)
    sine, cosine = jnp.sin(angles).T[0:8], jnp.cos(angles).T[0:8]
    s0, s1, c0, c1 = [
        jnp.broadcast_to(value[:, i : i + 1], (8, 128)) for value in (sine, cosine) for i in range(2)
    ]
    for copy in d_copies:
        copy.wait_recv()
    ordered = []
    for block in range(8):
        got = recv_d[block].astype(jnp.float32)
        grid = [[got[24 * i + 8 * j : 24 * i + 8 * j + 8] for j in range(3)] for i in range(3)]
        for j in range(3):
            e, n = grid[0][j], grid[1][j]
            grid[0][j], grid[1][j] = s0 * e + c0 * n, s0 * n - c0 * e
        for i in range(3):
            e, n = grid[i][0], grid[i][1]
            grid[i][0], grid[i][1] = s1 * e + c1 * n, s1 * n - c1 * e
        rotated = jnp.concatenate(grid[0] + grid[1] + grid[2] + [zero8], axis=0)
        ordered.append(rotated.astype(jnp.bfloat16).astype(jnp.float32))
    left0 = jnp.concatenate(ordered[0:2], axis=1).astype(jnp.bfloat16)
    left2 = jnp.concatenate(ordered[2:4], axis=1).astype(jnp.bfloat16)
    at_re = lanes((80, 128)) // 8 % 2 == 0
    turned = []
    for t in range(4, 8):
        re_part, im_part = pltpu.roll(ordered[t], 8, 1), pltpu.roll(ordered[t], 120, 1)
        turned.append(jnp.where(at_re, -im_part, re_part) if t < 6 else jnp.where(at_re, im_part, -re_part))
    left1 = jnp.concatenate(
        [jnp.concatenate(ordered[4:8], axis=1), jnp.concatenate(turned, axis=1)], axis=0
    ).astype(jnp.bfloat16)
    scale = 1.0 / math.sqrt(NF)
    for n in range(4):
        cols = slice(256 * n, 256 * n + 256)
        e0 = dot(left0, inv[0:256, cols])
        e2 = dot(left2, inv[256:512, cols])
        odd = dot(left1, inv[512:1024, cols])
        plus, minus = e0 + e2, e0 - e2
        odd_p, odd_n = odd[0:80], odd[80:160]
        for i, value in enumerate((plus + odd_p, minus + odd_n, plus - odd_p, minus - odd_n)):
            value = (value[0:72] * scale).reshape(9, 8, 256).astype(jnp.bfloat16)
            at = QUARTER * i + 256 * n
            out_ref[:, :, at : at + 256] = value

    for copy in pending:
        copy.wait_send()
    for i in range(8):
        pl.when(b != i)(to_owner(i).wait_send)


def on_device(records, station_row, pair_list, keep_mask, azimuth):
    forward, near, inverse = tables()
    own_pairs = azimuth.shape[1]
    bf16, f32 = jnp.bfloat16, jnp.float32
    dma = pltpu.SemaphoreType.DMA
    lagged = pl.pallas_call(
        kernel,
        out_shape=jax.ShapeDtypeStruct((9, own_pairs, NL), bf16),
        in_specs=[pl.BlockSpec(memory_space=pltpu.HBM)] * 8,
        out_specs=pl.BlockSpec(memory_space=pltpu.VMEM),
        scratch_shapes=[
            pltpu.VMEM(records.shape, bf16),
            pltpu.SMEM(station_row.shape, jnp.int32),
            pltpu.SMEM(pair_list.shape[::-1], jnp.int32),
            pltpu.VMEM(keep_mask.shape, jnp.int32),
            pltpu.VMEM(azimuth.shape, f32),
            pltpu.VMEM((24, NT), f32),
            pltpu.VMEM((QUARTER, 2 * NF), bf16),
            pltpu.VMEM((NF, NF), bf16),
            pltpu.VMEM((2 * NF, QUARTER), bf16),
            pltpu.VMEM((2, 8, 16, 128), bf16),
            pltpu.VMEM((2, 8, 16, 128), bf16),
            pltpu.VMEM((2, 8, 16, 128), bf16),
            pltpu.VMEM((2, 8, 16, 128), bf16),
            pltpu.VMEM((8, 192, 128), bf16),
            pltpu.VMEM((2, 192, 512), bf16),
            pltpu.VMEM((512, 1024), bf16),
            pltpu.VMEM((8, 80, 128), bf16),
            pltpu.VMEM((8, 80, 128), bf16),
            pltpu.VMEM((8, 80, 128), bf16),
            pltpu.VMEM((8, 80, 128), bf16),
            dma((8,)),
        ]
        + [dma((16,))] * 4
        + [dma((14,))] * 2
        + [dma((8,))] * 4,
        compiler_params=pltpu.CompilerParams(
            collective_id=0, has_side_effects=True, vmem_limit_bytes=48 << 20
        ),
        name="correlate",
    )(
        *[
            pltpu.with_memory_space_constraint(operand, pltpu.HBM)
            for operand in (records, station_row, pair_list.T, keep_mask, azimuth, forward, near, inverse)
        ]
    )
    return jnp.transpose(lagged, (1, 0, 2))


def solution(mesh):
    in_specs = (
        P("win", None, "blk", None),
        P(),
        P("blk", None),
        P("win", "blk"),
        P(None, ("blk", "win")),
    )
    out_specs = P(("blk", "win"), None, None)
    return jax.shard_map(
        on_device, mesh=mesh, in_specs=in_specs, out_specs=out_specs, check_vma=False
    )
```

```python
import math

import jax
import jax.numpy as jnp
import numpy as np
from jax import lax
from jax.experimental import pallas as pl
from jax.experimental.pallas import tpu as pltpu
from jax.sharding import PartitionSpec as P

NT = 4096
NF = 512
FLO = 16
SMOOTH = 11
NL = 4096
QUARTER = 1024
EPSILON = 1e-05

RESIDUE = (0, 0, 2, 2, 1, 1, 3, 3)
MESH = pl.DeviceIdType.MESH


def bin_order():
    place = np.arange(64)
    return np.stack([4 * ((block % 2) * 64 + place) + RESIDUE[block] for block in range(8)])


def tables():
    bins = bin_order()
    samples = np.arange(QUARTER)

    def phase(bin_ids, times):
        return (2.0 * math.pi / NT) * ((bin_ids[..., None] + FLO) * times % NT)

    ahead = phase(bins, samples)
    forward = np.concatenate([np.cos(ahead), -np.sin(ahead)], axis=1).reshape(2 * NF, QUARTER).T
    back = phase(bins, samples - NL // 2 + NT)
    back = back.reshape(8, 8, 8, QUARTER)
    inverse = np.stack([np.cos(back), -np.sin(back)], axis=2).reshape(2 * NF, QUARTER)
    flat = bins.reshape(-1)
    apart = np.abs(flat[:, None] - flat[None, :])
    near = np.minimum(apart, NF - apart) <= SMOOTH
    return (
        jnp.asarray(forward.astype(jnp.bfloat16)),
        jnp.asarray(near.astype(jnp.bfloat16)),
        jnp.asarray(inverse.astype(jnp.bfloat16)),
    )


def dot(left, right):
    return jnp.dot(left, right, preferred_element_type=jnp.float32)


def split(value):
    lead = value.astype(jnp.bfloat16).astype(jnp.float32)
    return jnp.concatenate([lead, value - lead], axis=0).astype(jnp.bfloat16)


def lanes(shape):
    return lax.broadcasted_iota(jnp.int32, shape, len(shape) - 1)


def swap_groups(vecs, group):
    vecs = list(vecs)
    lane_group = lanes(vecs[0].shape) // group
    for step in (1, 2, 4):
        high = (lane_group // step) % 2 == 1
        for i in range(8):
            if i & step:
                continue
            low_vec, high_vec = vecs[i], vecs[i + step]
            vecs[i] = jnp.where(high, pltpu.roll(high_vec, group * step, 1), low_vec)
            vecs[i + step] = jnp.where(high, high_vec, pltpu.roll(low_vec, 128 - group * step, 1))
    return vecs


def kernel(
    rec_hbm, station_hbm, pair_hbm, keep_hbm, angle_hbm, fwd_hbm, near_hbm, inv_hbm, out_ref,
    rec_ref, station_ref, pair_ref, keep_ref, angle_ref,
    rows32, fwd, near, inv, send_a, recv_a, send_b, recv_b, full, joined, onehot,
    send_c, recv_c, send_d, recv_d,
    tab_sem, a_s, a_r, b_s, b_r, z_s, z_r, c_s, c_r, d_s, d_r,
):
    blk = lax.axis_index("blk")
    win = lax.axis_index("win")
    y_hi, x = lax.div(blk, 64), lax.rem(lax.div(blk, 16), 4)
    z, core = lax.rem(lax.div(blk, 2), 8), lax.rem(blk, 2)
    a, b = x * 2 + core, y_hi * 4 + win

    at_a, at_b, at_z = {}, {}, {}
    for k in range(1, 8):
        other = lax.rem(a + k, 8)
        at_a[k] = other, (y_hi * 64 + lax.div(other, 2) * 16 + z * 2 + lax.rem(other, 2), win)
        other = lax.rem(b + k, 8)
        at_b[k] = other, (blk + (lax.div(other, 4) - y_hi) * 64, lax.rem(other, 4))
    for k in (1, 2, 6, 7):
        other = lax.rem(z + k, 8)
        at_z[k] = other, (blk + (other - z) * 2, win)

    loads = [
        pltpu.make_async_copy(src, dst, tab_sem.at[i])
        for i, (src, dst) in enumerate(
            (
                (rec_hbm, rec_ref),
                (fwd_hbm, fwd),
                (near_hbm, near),
                (keep_hbm, keep_ref),
                (station_hbm, station_ref),
                (pair_hbm, pair_ref),
                (angle_hbm, angle_ref),
                (inv_hbm, inv),
            )
        )
    ]
    barrier = pltpu.get_barrier_semaphore()
    for at in (at_z, at_b, at_a):
        for k in at:
            pl.semaphore_signal(barrier, inc=1, device_id=at[k][1], device_id_type=MESH)

    pending = []

    def send(src, dst, sem_s, sem_r, target):
        copy = pltpu.make_async_remote_copy(
            src_ref=src, dst_ref=dst, send_sem=sem_s, recv_sem=sem_r, device_id=target, device_id_type=MESH
        )
        copy.start()
        pending.append(copy)
        return copy

    for copy in loads[:7]:
        copy.start()

    for copy in loads[3:6]:
        copy.wait()
    lane8, lane16 = lanes((8, 128)), lanes((16, 128))
    row8 = lax.broadcasted_iota(jnp.int32, (8, 128), 0)
    zero8 = jnp.zeros((8, 128), jnp.float32)
    record = jnp.zeros((8, 128), jnp.int32)
    for p in range(8):
        for side in range(2):
            spot = jnp.logical_and(row8 == side, lane8 == p)
            record = jnp.where(spot, station_ref[pair_ref[side, win * 8 + p]], record)
    r_hi, r_x, r_z = record // 256, record // 64 % 4, record // 8 % 8
    r_c, r_s = record // 4 % 2, record % 4
    place = r_z * 64 + r_hi * 32 + (r_x * 2 + r_c) * 4 + r_s
    first_digit = (place // 16).astype(jnp.float32)
    second_digit = (place % 16).astype(jnp.float32)
    keep = jnp.concatenate([keep_ref[...].astype(jnp.float32), jnp.zeros((2, 96), jnp.float32)], axis=1)
    keep = jnp.concatenate([keep, jnp.zeros((6, 128), jnp.float32)], axis=0)
    digits = jnp.where(row8 < 6, pltpu.roll(first_digit, 4, 0), pltpu.roll(second_digit, 6, 0))
    own_table = (digits, pltpu.roll(keep, 4, 0))

    loads[0].wait()
    for w in range(2):
        for c in range(3):
            rows32[c * 8 + w * 4 : c * 8 + w * 4 + 4, :] = rec_ref[w, c].astype(jnp.float32)
    q0, q1, q2, q3 = [rows32[:, QUARTER * i : QUARTER * (i + 1)] for i in range(4)]
    s02, s13, d02, d13 = q0 + q2, q1 + q3, q0 - q2, q1 - q3
    left0, left2 = split(s02 + s13), split(s02 - s13)
    left1 = jnp.concatenate([split(d02), split(d13)], axis=0)

    loads[1].wait()
    got0 = dot(left0, fwd[:, 0:256])
    got2 = dot(left2, fwd[:, 256:512])
    got1 = dot(left1, fwd[:, 512:1024])
    even = jnp.concatenate([got0[:24] + got0[24:], got2[:24] + got2[24:]], axis=1)
    odd_a = got1[0:24] + got1[24:48]
    odd_b = got1[48:72] + got1[72:96]
    half = lanes((24, 128)) < 64
    spec = [even[:, 128 * t : 128 * t + 128] for t in range(4)]
    for t in range(4):
        turned = pltpu.roll(odd_b[:, 128 * t : 128 * t + 128], 64, 1)
        plus = half if t < 2 else jnp.logical_not(half)
        spec.append(odd_a[:, 128 * t : 128 * t + 128] + jnp.where(plus, turned, -turned))
    spec = [piece * (1.0 / math.sqrt(NT)) for piece in spec]

    low_half = row8 < 4
    half8 = lanes((8, 128)) < 64
    energy = []
    for piece in spec:
        square = piece * piece
        total = square[0:8] + square[8:16] + square[16:24]
        energy.append(total + pltpu.roll(total, 64, 1))
    energy = jnp.concatenate([jnp.where(half8, energy[2 * j], energy[2 * j + 1]) for j in range(4)], axis=1)
    loads[2].wait()
    smooth = dot(split(energy), near[...])
    smooth = smooth[0:8] + smooth[8:16]
    amp = lax.rsqrt(smooth / (3.0 * (2 * SMOOTH + 1)) + EPSILON)
    for t in range(8):
        piece = amp[:, 128 * (t // 2) : 128 * (t // 2) + 128]
        turned = pltpu.roll(piece, 64, 1)
        wide = jnp.where(half8, piece, turned) if t % 2 == 0 else jnp.where(half8, turned, piece)
        white = [spec[t][8 * c : 8 * c + 8] * wide for c in range(3)]
        for w in range(2):
            v0, v1, v2 = white if w == 0 else [pltpu.roll(value, 4, 0) for value in white]
            v1 = pltpu.roll(v1, 4, 0)
            chunk = [jnp.where(low_half, v0, v1), jnp.where(low_half, v2, own_table[w])]
            send_a[w, t] = jnp.concatenate(chunk, axis=0).astype(jnp.bfloat16)

    pl.semaphore_wait(barrier, 18)

    far_first = (4, 3, 5, 2, 6, 1, 7)
    a_copies = [[], []]
    for w in range(2):
        for k in far_first:
            other, target = at_a[k]
            a_copies[w].append(
                send(send_a.at[w, other], recv_a.at[w, a], a_s.at[8 * w + k], a_r.at[8 * w + k], target)
            )
        recv_a[w, a] = send_a[w, a]
    loads[7].start()

    b_copies = [[], []]
    for w in range(2):
        for copy in a_copies[w]:
            copy.wait_recv()
        got = [recv_a[w, i].astype(jnp.float32) for i in range(8)]
        tops, lows = [value[0:8] for value in got], [value[8:16] for value in got]
        stacked = []
        for c in range(3):
            parts = tops if c < 2 else lows
            for j in range(4):
                first, second = parts[2 * j], parts[2 * j + 1]
                if c == 1:
                    stacked.append(jnp.where(low_half, pltpu.roll(first, 4, 0), second))
                else:
                    stacked.append(jnp.where(low_half, first, pltpu.roll(second, 4, 0)))
        stacked += [zero8] * 4
        turn = jnp.concatenate(stacked, axis=0).T

        def spread(a_half, q):
            merged = zero8
            for i in range(4):
                piece = pltpu.roll(lows[4 * a_half + i], (96 + 8 * i - 8 * q) % 128, 1)
                merged = jnp.where(lane8 // 8 == 12 + i, piece, merged)
            return merged

        if w == 0:
            tail = [jnp.where(low_half, pltpu.roll(spread(0, 0), 4, 0), spread(1, 0)), zero8]
        else:
            tail = []
            for a_half in range(2):
                merged = zero8
                for q in range(4):
                    piece = spread(a_half, q)
                    piece = piece if q == 2 else pltpu.roll(piece, (2 * q + 4) % 8, 0)
                    merged = jnp.where(row8 // 2 == q, piece, merged)
                tail.append(merged)
        for i in range(8):
            send_b[w, i] = jnp.concatenate(
                [turn[8 * i : 8 * i + 8] + tail[0], turn[64 + 8 * i : 72 + 8 * i] + tail[1]], axis=0
            ).astype(jnp.bfloat16)
        for k in far_first:
            other, target = at_b[k]
            b_copies[w].append(
                send(send_b.at[w, other], recv_b.at[w, b], b_s.at[8 * w + k], b_r.at[8 * w + k], target)
            )
        recv_b[w, b] = send_b[w, b]

    def share(source, h, k, sem):
        block = full.at[source, pl.ds(96 * h, 96)]
        return send(block, block, z_s.at[sem], z_r.at[sem], at_z[k][1])

    direct = {}
    tables_got = []
    for w in range(2):
        for copy in b_copies[w]:
            copy.wait_recv()
        got = [recv_b[w, i].astype(jnp.float32) for i in range(8)]
        mine = []
        for odd in range(2):
            for c in range(3):
                out = None
                for j in range(4):
                    piece = got[4 * (j % 2) + 2 * (j // 2) + odd]
                    shift = (32 * (j - c)) % 128
                    piece = pltpu.roll(piece, shift, 1) if shift else piece
                    out = piece if out is None else jnp.where(lane16 // 32 == j, piece, out)
                mine.append(out)
        full[z, 96 * w : 96 * w + 96] = jnp.concatenate(mine, axis=0).astype(jnp.bfloat16)
        for k in (2, 6):
            direct[k, w] = share(z, w, k, len(direct))
        table = []
        for t in range(4):
            merged = zero8
            for j in range(4):
                shift = (32 + 32 * j) % 128
                here = lane8 // 32 == j
                if w == 0:
                    piece = got[2 * t + j // 2][0:8]
                    piece = pltpu.roll(piece, 4, 0) if j % 2 else piece
                    piece = pltpu.roll(piece, shift, 1) if shift else piece
                    merged = jnp.where(here, piece, merged)
                    continue
                for q in range(4):
                    piece = got[4 * (t // 2) + q][8 * (j % 2) : 8 * (j % 2) + 8]
                    down = (2 * q - 2 * (2 * t % 4 + j // 2)) % 8
                    piece = pltpu.roll(piece, down, 0) if down else piece
                    piece = pltpu.roll(piece, shift, 1) if shift else piece
                    merged = jnp.where(jnp.logical_and(here, row8 // 2 == q), piece, merged)
            table.append(merged)
        tables_got.append(table)
    z_copies = []
    for w in range(2):
        for k in (1, 7):
            direct[k, w] = share(z, w, k, len(direct))
            z_copies.append(direct[k, w])
    info, keeps = tables_got

    place_ids = lax.broadcasted_iota(jnp.int32, (512, 128), 0)
    for t in range(4):
        for side in range(2):
            place = (16.0 * info[t][side : side + 1] + info[t][2 + side : 3 + side]).astype(jnp.int32)
            at = 256 * t + 128 * side
            onehot[:, at : at + 128] = jnp.where(place_ids == place, 1.0, 0.0).astype(jnp.bfloat16)

    for h in range(2):
        for step, (k, near_k) in enumerate(((2, 1), (6, 7))):
            direct[k, h].wait_recv()
            source = at_z[8 - k][0]
            z_copies.append(share(source, h, near_k, 10 + 2 * h + step))
            if h == step:
                z_copies.append(share(source, h, k, 8 + step))
    for copy in z_copies:
        copy.wait_recv()

    def to_owner(i):
        return pltpu.make_async_remote_copy(
            src_ref=send_c.at[i],
            dst_ref=recv_c.at[b],
            send_sem=c_s.at[i],
            recv_sem=c_r.at[b],
            device_id=(blk + (i // 4 - y_hi) * 64, i % 4),
            device_id_type=MESH,
        )

    def from_source(i):
        return pltpu.make_async_remote_copy(
            src_ref=send_c.at[i],
            dst_ref=recv_c.at[i],
            send_sem=c_s.at[i],
            recv_sem=c_r.at[i],
            device_id=(blk + (i // 4 - y_hi) * 64, i % 4),
            device_id_type=MESH,
        )

    low_lanes = lanes((192, 128)) < 64
    for j in range(4):
        first, second = full[2 * j].astype(jnp.float32), full[2 * j + 1].astype(jnp.float32)
        cols = slice(128 * j, 128 * j + 128)
        joined[0, :, cols] = jnp.where(low_lanes, first, pltpu.roll(second, 64, 1)).astype(jnp.bfloat16)
        joined[1, :, cols] = jnp.where(low_lanes, pltpu.roll(first, 64, 1), second).astype(jnp.bfloat16)
    for t in range(4):
        halves = [dot(joined[i], onehot[:, 256 * t : 256 * t + 256]) for i in range(2)]
        re = [[None] * 3 for _ in range(3)]
        im = [[None] * 3 for _ in range(3)]
        for w in range(8):
            mask = jnp.broadcast_to(keeps[t][w : w + 1], (8, 128))
            both = halves[w // 4]
            base = 96 * (w % 2) + 48 * (w // 2 % 2)

            def part(c, ri, side):
                at = base + 16 * c + 8 * ri
                return both[at : at + 8, 128 * side : 128 * side + 128]

            first = [(part(c, 0, 0) * mask, part(c, 1, 0) * mask) for c in range(3)]
            second = [(part(c, 0, 1), part(c, 1, 1)) for c in range(3)]
            for c in range(3):
                for d in range(3):
                    ar, ai = first[c]
                    br, bi = second[d]
                    new_re, new_im = ar * br + ai * bi, ai * br - ar * bi
                    re[c][d] = new_re if w == 0 else re[c][d] + new_re
                    im[c][d] = new_im if w == 0 else im[c][d] + new_im
        flat = []
        for i in range(3):
            for j in range(3):
                flat += [re[i][j], im[i][j]]
        main = jnp.concatenate(flat[:16], axis=0).T
        rest = jnp.concatenate(flat[16:], axis=0).T
        rest = jnp.concatenate([rest, jnp.zeros((128, 112), jnp.float32)], axis=1)
        for half_id in range(2):
            packed = jnp.zeros((8, 128), jnp.float32)
            for i in range(8):
                piece = rest[64 * half_id + 8 * i : 64 * half_id + 8 * i + 8]
                piece = pltpu.roll(piece, 16 * i, 1) if i else piece
                packed = jnp.where(lane8 // 16 == i, piece, packed)
            send_c[2 * t + half_id] = jnp.concatenate(
                [main[64 * half_id : 64 * half_id + 64], packed, jnp.zeros((8, 128), jnp.float32)], axis=0
            ).astype(jnp.bfloat16)
            pl.when(b != 2 * t + half_id)(to_owner(2 * t + half_id).start)

    recv_c[b] = send_c[b]
    for i in range(8):
        pl.when(b != i)(from_source(i).wait_recv)
    rest = swap_groups([recv_c[i, 64:80].astype(jnp.float32)[0:8] for i in range(8)], 16)
    for pair in range(4):
        pieces = [recv_c[i, 16 * pair : 16 * pair + 16].astype(jnp.float32) for i in range(8)]
        swapped = swap_groups(pieces, 16)
        for j in range(2):
            send_d[2 * pair + j] = jnp.concatenate(
                [piece[8 * j : 8 * j + 8] for piece in swapped]
                + [rest[2 * pair + j], jnp.zeros((8, 128), jnp.float32)],
                axis=0,
            ).astype(jnp.bfloat16)
    d_copies = []
    for k in (4, 3, 5, 2, 6, 1, 7):
        other, target = at_a[k]
        d_copies.append(send(send_d.at[other], recv_d.at[a], d_s.at[k], d_r.at[k], target))
    recv_d[a] = send_d[a]

    loads[7].wait()
    loads[6].wait()
    angles = jnp.concatenate([angle_ref[...], jnp.zeros((2, 120), jnp.float32)], axis=1)
    angles = jnp.concatenate([angles, jnp.zeros((6, 128), jnp.float32)], axis=0)
    sine, cosine = jnp.sin(angles).T[0:8], jnp.cos(angles).T[0:8]
    s0, s1, c0, c1 = [
        jnp.broadcast_to(value[:, i : i + 1], (8, 128)) for value in (sine, cosine) for i in range(2)
    ]
    for copy in d_copies:
        copy.wait_recv()
    ordered = []
    for block in range(8):
        got = recv_d[block].astype(jnp.float32)
        grid = [[got[24 * i + 8 * j : 24 * i + 8 * j + 8] for j in range(3)] for i in range(3)]
        for j in range(3):
            e, n = grid[0][j], grid[1][j]
            grid[0][j], grid[1][j] = s0 * e + c0 * n, s0 * n - c0 * e
        for i in range(3):
            e, n = grid[i][0], grid[i][1]
            grid[i][0], grid[i][1] = s1 * e + c1 * n, s1 * n - c1 * e
        rotated = jnp.concatenate(grid[0] + grid[1] + grid[2] + [zero8], axis=0)
        ordered.append(rotated.astype(jnp.bfloat16).astype(jnp.float32))
    left0 = jnp.concatenate(ordered[0:2], axis=1).astype(jnp.bfloat16)
    left2 = jnp.concatenate(ordered[2:4], axis=1).astype(jnp.bfloat16)
    at_re = lanes((80, 128)) // 8 % 2 == 0
    turned = []
    for t in range(4, 8):
        re_part, im_part = pltpu.roll(ordered[t], 8, 1), pltpu.roll(ordered[t], 120, 1)
        turned.append(jnp.where(at_re, -im_part, re_part) if t < 6 else jnp.where(at_re, im_part, -re_part))
    left1 = jnp.concatenate(
        [jnp.concatenate(ordered[4:8], axis=1), jnp.concatenate(turned, axis=1)], axis=0
    ).astype(jnp.bfloat16)
    scale = 1.0 / math.sqrt(NF)
    for n in range(4):
        cols = slice(256 * n, 256 * n + 256)
        e0 = dot(left0, inv[0:256, cols])
        e2 = dot(left2, inv[256:512, cols])
        odd = dot(left1, inv[512:1024, cols])
        plus, minus = e0 + e2, e0 - e2
        odd_p, odd_n = odd[0:80], odd[80:160]
        for i, value in enumerate((plus + odd_p, minus + odd_n, plus - odd_p, minus - odd_n)):
            value = (value[0:72] * scale).reshape(9, 8, 256).astype(jnp.bfloat16)
            at = QUARTER * i + 256 * n
            out_ref[:, :, at : at + 256] = value

    for copy in pending:
        copy.wait_send()
    for i in range(8):
        pl.when(b != i)(to_owner(i).wait_send)


def on_device(records, station_row, pair_list, keep_mask, azimuth):
    forward, near, inverse = tables()
    own_pairs = azimuth.shape[1]
    bf16, f32 = jnp.bfloat16, jnp.float32
    dma = pltpu.SemaphoreType.DMA
    lagged = pl.pallas_call(
        kernel,
        out_shape=jax.ShapeDtypeStruct((9, own_pairs, NL), bf16),
        in_specs=[pl.BlockSpec(memory_space=pltpu.HBM)] * 8,
        out_specs=pl.BlockSpec(memory_space=pltpu.VMEM),
        scratch_shapes=[
            pltpu.VMEM(records.shape, bf16),
            pltpu.SMEM(station_row.shape, jnp.int32),
            pltpu.SMEM(pair_list.shape[::-1], jnp.int32),
            pltpu.VMEM(keep_mask.shape, jnp.int32),
            pltpu.VMEM(azimuth.shape, f32),
            pltpu.VMEM((24, NT), f32),
            pltpu.VMEM((QUARTER, 2 * NF), bf16),
            pltpu.VMEM((NF, NF), bf16),
            pltpu.VMEM((2 * NF, QUARTER), bf16),
            pltpu.VMEM((2, 8, 16, 128), bf16),
            pltpu.VMEM((2, 8, 16, 128), bf16),
            pltpu.VMEM((2, 8, 16, 128), bf16),
            pltpu.VMEM((2, 8, 16, 128), bf16),
            pltpu.VMEM((8, 192, 128), bf16),
            pltpu.VMEM((2, 192, 512), bf16),
            pltpu.VMEM((512, 1024), bf16),
            pltpu.VMEM((8, 80, 128), bf16),
            pltpu.VMEM((8, 80, 128), bf16),
            pltpu.VMEM((8, 80, 128), bf16),
            pltpu.VMEM((8, 80, 128), bf16),
            dma((8,)),
        ]
        + [dma((16,))] * 4
        + [dma((14,))] * 2
        + [dma((8,))] * 4,
        compiler_params=pltpu.CompilerParams(
            collective_id=0, has_side_effects=True, vmem_limit_bytes=48 << 20
        ),
        name="correlate",
    )(
        *[
            pltpu.with_memory_space_constraint(operand, pltpu.HBM)
            for operand in (records, station_row, pair_list.T, keep_mask, azimuth, forward, near, inverse)
        ]
    )
    return jnp.transpose(lagged, (1, 0, 2))


def solution(mesh):
    in_specs = (
        P("win", None, "blk", None),
        P(),
        P("blk", None),
        P("win", "blk"),
        P(None, ("blk", "win")),
    )
    out_specs = P(("blk", "win"), None, None)
    return jax.shard_map(
        on_device, mesh=mesh, in_specs=in_specs, out_specs=out_specs, check_vma=False
    )
```

```python
import math

import jax
import jax.numpy as jnp
import numpy as np
from jax import lax
from jax.experimental import pallas as pl
from jax.experimental.pallas import tpu as pltpu
from jax.sharding import PartitionSpec as P

NT = 4096
NF = 512
FLO = 16
SMOOTH = 11
NL = 4096
QUARTER = 1024
EPSILON = 1e-05

RESIDUE = (0, 0, 2, 2, 1, 1, 3, 3)
MESH = pl.DeviceIdType.MESH


def bin_order():
    place = np.arange(64)
    return np.stack([4 * ((block % 2) * 64 + place) + RESIDUE[block] for block in range(8)])


def tables():
    bins = bin_order()
    samples = np.arange(QUARTER)

    def phase(bin_ids, times):
        return (2.0 * math.pi / NT) * ((bin_ids[..., None] + FLO) * times % NT)

    ahead = phase(bins, samples)
    forward = np.concatenate([np.cos(ahead), -np.sin(ahead)], axis=1).reshape(2 * NF, QUARTER).T
    back = phase(bins, samples - NL // 2 + NT)
    back = back.reshape(8, 8, 8, QUARTER)
    inverse = np.stack([np.cos(back), -np.sin(back)], axis=2).reshape(2 * NF, QUARTER)
    flat = bins.reshape(-1)
    apart = np.abs(flat[:, None] - flat[None, :])
    near = np.minimum(apart, NF - apart) <= SMOOTH
    return (
        jnp.asarray(forward.astype(jnp.bfloat16)),
        jnp.asarray(near.astype(jnp.bfloat16)),
        jnp.asarray(inverse.astype(jnp.bfloat16)),
    )


def dot(left, right):
    return jnp.dot(left, right, preferred_element_type=jnp.float32)


def split(value):
    lead = value.astype(jnp.bfloat16).astype(jnp.float32)
    return jnp.concatenate([lead, value - lead], axis=0).astype(jnp.bfloat16)


def lanes(shape):
    return lax.broadcasted_iota(jnp.int32, shape, len(shape) - 1)


def swap_groups(vecs, group):
    vecs = list(vecs)
    lane_group = lanes(vecs[0].shape) // group
    for step in (1, 2, 4):
        high = (lane_group // step) % 2 == 1
        for i in range(8):
            if i & step:
                continue
            low_vec, high_vec = vecs[i], vecs[i + step]
            vecs[i] = jnp.where(high, pltpu.roll(high_vec, group * step, 1), low_vec)
            vecs[i + step] = jnp.where(high, high_vec, pltpu.roll(low_vec, 128 - group * step, 1))
    return vecs


def kernel(
    rec_hbm, station_hbm, pair_hbm, keep_hbm, angle_hbm, fwd_hbm, near_hbm, inv_hbm, out_ref,
    rec_ref, station_ref, pair_ref, keep_ref, angle_ref,
    rows32, fwd, near, inv, send_a, recv_a, send_b, recv_b, full, joined, onehot,
    send_c, recv_c, send_d, recv_d,
    tab_sem, a_s, a_r, b_s, b_r, z_s, z_r, c_s, c_r, d_s, d_r,
):
    blk = lax.axis_index("blk")
    win = lax.axis_index("win")
    y_hi, x = lax.div(blk, 64), lax.rem(lax.div(blk, 16), 4)
    z, core = lax.rem(lax.div(blk, 2), 8), lax.rem(blk, 2)
    a, b = x * 2 + core, y_hi * 4 + win

    at_a, at_b, at_z = {}, {}, {}
    for k in range(1, 8):
        other = lax.rem(a + k, 8)
        at_a[k] = other, (y_hi * 64 + lax.div(other, 2) * 16 + z * 2 + lax.rem(other, 2), win)
        other = lax.rem(b + k, 8)
        at_b[k] = other, (blk + (lax.div(other, 4) - y_hi) * 64, lax.rem(other, 4))
    for k in (1, 2, 6, 7):
        other = lax.rem(z + k, 8)
        at_z[k] = other, (blk + (other - z) * 2, win)

    loads = [
        pltpu.make_async_copy(src, dst, tab_sem.at[i])
        for i, (src, dst) in enumerate(
            (
                (rec_hbm, rec_ref),
                (fwd_hbm, fwd),
                (near_hbm, near),
                (keep_hbm, keep_ref),
                (station_hbm, station_ref),
                (pair_hbm, pair_ref),
                (angle_hbm, angle_ref),
                (inv_hbm, inv),
            )
        )
    ]
    barrier = pltpu.get_barrier_semaphore()
    for at in (at_z, at_b, at_a):
        for k in at:
            pl.semaphore_signal(barrier, inc=1, device_id=at[k][1], device_id_type=MESH)

    pending = []

    def send(src, dst, sem_s, sem_r, target):
        copy = pltpu.make_async_remote_copy(
            src_ref=src, dst_ref=dst, send_sem=sem_s, recv_sem=sem_r, device_id=target, device_id_type=MESH
        )
        copy.start()
        pending.append(copy)
        return copy

    for copy in loads[:7]:
        copy.start()

    for copy in loads[3:6]:
        copy.wait()
    lane8, lane16 = lanes((8, 128)), lanes((16, 128))
    row8 = lax.broadcasted_iota(jnp.int32, (8, 128), 0)
    zero8 = jnp.zeros((8, 128), jnp.float32)
    record = jnp.zeros((8, 128), jnp.int32)
    for p in range(8):
        for side in range(2):
            spot = jnp.logical_and(row8 == side, lane8 == p)
            record = jnp.where(spot, station_ref[pair_ref[side, win * 8 + p]], record)
    r_hi, r_x, r_z = record // 256, record // 64 % 4, record // 8 % 8
    r_c, r_s = record // 4 % 2, record % 4
    place = r_z * 64 + r_hi * 32 + (r_x * 2 + r_c) * 4 + r_s
    first_digit = (place // 16).astype(jnp.float32)
    second_digit = (place % 16).astype(jnp.float32)
    keep = jnp.concatenate([keep_ref[...].astype(jnp.float32), jnp.zeros((2, 96), jnp.float32)], axis=1)
    keep = jnp.concatenate([keep, jnp.zeros((6, 128), jnp.float32)], axis=0)
    digits = jnp.where(row8 < 6, pltpu.roll(first_digit, 4, 0), pltpu.roll(second_digit, 6, 0))
    own_table = (digits, pltpu.roll(keep, 4, 0))

    loads[0].wait()
    for w in range(2):
        for c in range(3):
            rows32[c * 8 + w * 4 : c * 8 + w * 4 + 4, :] = rec_ref[w, c].astype(jnp.float32)
    q0, q1, q2, q3 = [rows32[:, QUARTER * i : QUARTER * (i + 1)] for i in range(4)]
    s02, s13, d02, d13 = q0 + q2, q1 + q3, q0 - q2, q1 - q3
    left0, left2 = split(s02 + s13), split(s02 - s13)
    left1 = jnp.concatenate([split(d02), split(d13)], axis=0)

    loads[1].wait()
    got0 = dot(left0, fwd[:, 0:256])
    got2 = dot(left2, fwd[:, 256:512])
    got1 = dot(left1, fwd[:, 512:1024])
    even = jnp.concatenate([got0[:24] + got0[24:], got2[:24] + got2[24:]], axis=1)
    odd_a = got1[0:24] + got1[24:48]
    odd_b = got1[48:72] + got1[72:96]
    half = lanes((24, 128)) < 64
    spec = [even[:, 128 * t : 128 * t + 128] for t in range(4)]
    for t in range(4):
        turned = pltpu.roll(odd_b[:, 128 * t : 128 * t + 128], 64, 1)
        plus = half if t < 2 else jnp.logical_not(half)
        spec.append(odd_a[:, 128 * t : 128 * t + 128] + jnp.where(plus, turned, -turned))
    spec = [piece * (1.0 / math.sqrt(NT)) for piece in spec]

    low_half = row8 < 4
    half8 = lanes((8, 128)) < 64
    energy = []
    for piece in spec:
        square = piece * piece
        total = square[0:8] + square[8:16] + square[16:24]
        energy.append(total + pltpu.roll(total, 64, 1))
    energy = jnp.concatenate([jnp.where(half8, energy[2 * j], energy[2 * j + 1]) for j in range(4)], axis=1)
    loads[2].wait()
    smooth = dot(split(energy), near[...])
    smooth = smooth[0:8] + smooth[8:16]
    amp = lax.rsqrt(smooth / (3.0 * (2 * SMOOTH + 1)) + EPSILON)
    for t in range(8):
        piece = amp[:, 128 * (t // 2) : 128 * (t // 2) + 128]
        turned = pltpu.roll(piece, 64, 1)
        wide = jnp.where(half8, piece, turned) if t % 2 == 0 else jnp.where(half8, turned, piece)
        white = [spec[t][8 * c : 8 * c + 8] * wide for c in range(3)]
        for w in range(2):
            v0, v1, v2 = white if w == 0 else [pltpu.roll(value, 4, 0) for value in white]
            v1 = pltpu.roll(v1, 4, 0)
            chunk = [jnp.where(low_half, v0, v1), jnp.where(low_half, v2, own_table[w])]
            send_a[w, t] = jnp.concatenate(chunk, axis=0).astype(jnp.bfloat16)

    pl.semaphore_wait(barrier, 18)

    far_first = (4, 3, 5, 2, 6, 1, 7)
    a_copies = [[], []]
    for w in range(2):
        for k in far_first:
            other, target = at_a[k]
            a_copies[w].append(
                send(send_a.at[w, other], recv_a.at[w, a], a_s.at[8 * w + k], a_r.at[8 * w + k], target)
            )
        recv_a[w, a] = send_a[w, a]
    loads[7].start()

    b_copies = [[], []]
    for w in range(2):
        for copy in a_copies[w]:
            copy.wait_recv()
        got = [recv_a[w, i].astype(jnp.float32) for i in range(8)]
        tops, lows = [value[0:8] for value in got], [value[8:16] for value in got]
        stacked = []
        for c in range(3):
            parts = tops if c < 2 else lows
            for j in range(4):
                first, second = parts[2 * j], parts[2 * j + 1]
                if c == 1:
                    stacked.append(jnp.where(low_half, pltpu.roll(first, 4, 0), second))
                else:
                    stacked.append(jnp.where(low_half, first, pltpu.roll(second, 4, 0)))
        stacked += [zero8] * 4
        turn = jnp.concatenate(stacked, axis=0).T

        def spread(a_half, q):
            merged = zero8
            for i in range(4):
                piece = pltpu.roll(lows[4 * a_half + i], (96 + 8 * i - 8 * q) % 128, 1)
                merged = jnp.where(lane8 // 8 == 12 + i, piece, merged)
            return merged

        if w == 0:
            tail = [jnp.where(low_half, pltpu.roll(spread(0, 0), 4, 0), spread(1, 0)), zero8]
        else:
            tail = []
            for a_half in range(2):
                merged = zero8
                for q in range(4):
                    piece = spread(a_half, q)
                    piece = piece if q == 2 else pltpu.roll(piece, (2 * q + 4) % 8, 0)
                    merged = jnp.where(row8 // 2 == q, piece, merged)
                tail.append(merged)
        for i in range(8):
            send_b[w, i] = jnp.concatenate(
                [turn[8 * i : 8 * i + 8] + tail[0], turn[64 + 8 * i : 72 + 8 * i] + tail[1]], axis=0
            ).astype(jnp.bfloat16)
        for k in far_first:
            other, target = at_b[k]
            b_copies[w].append(
                send(send_b.at[w, other], recv_b.at[w, b], b_s.at[8 * w + k], b_r.at[8 * w + k], target)
            )
        recv_b[w, b] = send_b[w, b]

    def share(source, h, k, sem):
        block = full.at[source, pl.ds(96 * h, 96)]
        return send(block, block, z_s.at[sem], z_r.at[sem], at_z[k][1])

    direct = {}
    tables_got = []
    for w in range(2):
        for copy in b_copies[w]:
            copy.wait_recv()
        got = [recv_b[w, i].astype(jnp.float32) for i in range(8)]
        mine = []
        for odd in range(2):
            for c in range(3):
                out = None
                for j in range(4):
                    piece = got[4 * (j % 2) + 2 * (j // 2) + odd]
                    shift = (32 * (j - c)) % 128
                    piece = pltpu.roll(piece, shift, 1) if shift else piece
                    out = piece if out is None else jnp.where(lane16 // 32 == j, piece, out)
                mine.append(out)
        full[z, 96 * w : 96 * w + 96] = jnp.concatenate(mine, axis=0).astype(jnp.bfloat16)
        for k in (2, 6):
            direct[k, w] = share(z, w, k, len(direct))
        if w == 1:
            z_copies = [share(z, h, k, 4 + 2 * h + side) for h in range(2) for side, k in enumerate((1, 7))]
        table = []
        for t in range(4):
            merged = zero8
            for j in range(4):
                shift = (32 + 32 * j) % 128
                here = lane8 // 32 == j
                if w == 0:
                    piece = got[2 * t + j // 2][0:8]
                    piece = pltpu.roll(piece, 4, 0) if j % 2 else piece
                    piece = pltpu.roll(piece, shift, 1) if shift else piece
                    merged = jnp.where(here, piece, merged)
                    continue
                for q in range(4):
                    piece = got[4 * (t // 2) + q][8 * (j % 2) : 8 * (j % 2) + 8]
                    down = (2 * q - 2 * (2 * t % 4 + j // 2)) % 8
                    piece = pltpu.roll(piece, down, 0) if down else piece
                    piece = pltpu.roll(piece, shift, 1) if shift else piece
                    merged = jnp.where(jnp.logical_and(here, row8 // 2 == q), piece, merged)
            table.append(merged)
        tables_got.append(table)
    info, keeps = tables_got

    for h in range(2):
        for step, (k, near_k) in enumerate(((2, 1), (6, 7))):
            direct[k, h].wait_recv()
            source = at_z[8 - k][0]
            z_copies.append(share(source, h, near_k, 10 + 2 * h + step))
            if h == step:
                z_copies.append(share(source, h, k, 8 + step))
    place_ids = lax.broadcasted_iota(jnp.int32, (512, 128), 0)
    for t in range(4):
        for side in range(2):
            place = (16.0 * info[t][side : side + 1] + info[t][2 + side : 3 + side]).astype(jnp.int32)
            at = 256 * t + 128 * side
            onehot[:, at : at + 128] = jnp.where(place_ids == place, 1.0, 0.0).astype(jnp.bfloat16)

    for copy in z_copies:
        copy.wait_recv()

    def to_owner(i):
        return pltpu.make_async_remote_copy(
            src_ref=send_c.at[i],
            dst_ref=recv_c.at[b],
            send_sem=c_s.at[i],
            recv_sem=c_r.at[b],
            device_id=(blk + (i // 4 - y_hi) * 64, i % 4),
            device_id_type=MESH,
        )

    def from_source(i):
        return pltpu.make_async_remote_copy(
            src_ref=send_c.at[i],
            dst_ref=recv_c.at[i],
            send_sem=c_s.at[i],
            recv_sem=c_r.at[i],
            device_id=(blk + (i // 4 - y_hi) * 64, i % 4),
            device_id_type=MESH,
        )

    low_lanes = lanes((192, 128)) < 64
    for j in range(4):
        first, second = full[2 * j].astype(jnp.float32), full[2 * j + 1].astype(jnp.float32)
        cols = slice(128 * j, 128 * j + 128)
        joined[0, :, cols] = jnp.where(low_lanes, first, pltpu.roll(second, 64, 1)).astype(jnp.bfloat16)
        joined[1, :, cols] = jnp.where(low_lanes, pltpu.roll(first, 64, 1), second).astype(jnp.bfloat16)
    for t in range(4):
        halves = [dot(joined[i], onehot[:, 256 * t : 256 * t + 256]) for i in range(2)]
        re = [[None] * 3 for _ in range(3)]
        im = [[None] * 3 for _ in range(3)]
        for w in range(8):
            mask = jnp.broadcast_to(keeps[t][w : w + 1], (8, 128))
            both = halves[w // 4]
            base = 96 * (w % 2) + 48 * (w // 2 % 2)

            def part(c, ri, side):
                at = base + 16 * c + 8 * ri
                return both[at : at + 8, 128 * side : 128 * side + 128]

            first = [(part(c, 0, 0) * mask, part(c, 1, 0) * mask) for c in range(3)]
            second = [(part(c, 0, 1), part(c, 1, 1)) for c in range(3)]
            for c in range(3):
                for d in range(3):
                    ar, ai = first[c]
                    br, bi = second[d]
                    new_re, new_im = ar * br + ai * bi, ai * br - ar * bi
                    re[c][d] = new_re if w == 0 else re[c][d] + new_re
                    im[c][d] = new_im if w == 0 else im[c][d] + new_im
        flat = []
        for i in range(3):
            for j in range(3):
                flat += [re[i][j], im[i][j]]
        main = jnp.concatenate(flat[:16], axis=0).T
        rest = jnp.concatenate(flat[16:], axis=0).T
        rest = jnp.concatenate([rest, jnp.zeros((128, 112), jnp.float32)], axis=1)
        for half_id in range(2):
            packed = jnp.zeros((8, 128), jnp.float32)
            for i in range(8):
                piece = rest[64 * half_id + 8 * i : 64 * half_id + 8 * i + 8]
                piece = pltpu.roll(piece, 16 * i, 1) if i else piece
                packed = jnp.where(lane8 // 16 == i, piece, packed)
            send_c[2 * t + half_id] = jnp.concatenate(
                [main[64 * half_id : 64 * half_id + 64], packed, jnp.zeros((8, 128), jnp.float32)], axis=0
            ).astype(jnp.bfloat16)
            pl.when(b != 2 * t + half_id)(to_owner(2 * t + half_id).start)

    recv_c[b] = send_c[b]
    for i in range(8):
        pl.when(b != i)(from_source(i).wait_recv)
    rest = swap_groups([recv_c[i, 64:80].astype(jnp.float32)[0:8] for i in range(8)], 16)
    for pair in range(4):
        pieces = [recv_c[i, 16 * pair : 16 * pair + 16].astype(jnp.float32) for i in range(8)]
        swapped = swap_groups(pieces, 16)
        for j in range(2):
            send_d[2 * pair + j] = jnp.concatenate(
                [piece[8 * j : 8 * j + 8] for piece in swapped]
                + [rest[2 * pair + j], jnp.zeros((8, 128), jnp.float32)],
                axis=0,
            ).astype(jnp.bfloat16)
    d_copies = []
    for k in (4, 3, 5, 2, 6, 1, 7):
        other, target = at_a[k]
        d_copies.append(send(send_d.at[other], recv_d.at[a], d_s.at[k], d_r.at[k], target))
    recv_d[a] = send_d[a]

    loads[7].wait()
    loads[6].wait()
    angles = jnp.concatenate([angle_ref[...], jnp.zeros((2, 120), jnp.float32)], axis=1)
    angles = jnp.concatenate([angles, jnp.zeros((6, 128), jnp.float32)], axis=0)
    sine, cosine = jnp.sin(angles).T[0:8], jnp.cos(angles).T[0:8]
    s0, s1, c0, c1 = [
        jnp.broadcast_to(value[:, i : i + 1], (8, 128)) for value in (sine, cosine) for i in range(2)
    ]
    for copy in d_copies:
        copy.wait_recv()
    ordered = []
    for block in range(8):
        got = recv_d[block].astype(jnp.float32)
        grid = [[got[24 * i + 8 * j : 24 * i + 8 * j + 8] for j in range(3)] for i in range(3)]
        for j in range(3):
            e, n = grid[0][j], grid[1][j]
            grid[0][j], grid[1][j] = s0 * e + c0 * n, s0 * n - c0 * e
        for i in range(3):
            e, n = grid[i][0], grid[i][1]
            grid[i][0], grid[i][1] = s1 * e + c1 * n, s1 * n - c1 * e
        rotated = jnp.concatenate(grid[0] + grid[1] + grid[2] + [zero8], axis=0)
        ordered.append(rotated.astype(jnp.bfloat16).astype(jnp.float32))
    left0 = jnp.concatenate(ordered[0:2], axis=1).astype(jnp.bfloat16)
    left2 = jnp.concatenate(ordered[2:4], axis=1).astype(jnp.bfloat16)
    at_re = lanes((80, 128)) // 8 % 2 == 0
    turned = []
    for t in range(4, 8):
        re_part, im_part = pltpu.roll(ordered[t], 8, 1), pltpu.roll(ordered[t], 120, 1)
        turned.append(jnp.where(at_re, -im_part, re_part) if t < 6 else jnp.where(at_re, im_part, -re_part))
    left1 = jnp.concatenate(
        [jnp.concatenate(ordered[4:8], axis=1), jnp.concatenate(turned, axis=1)], axis=0
    ).astype(jnp.bfloat16)
    scale = 1.0 / math.sqrt(NF)
    for n in range(4):
        cols = slice(256 * n, 256 * n + 256)
        e0 = dot(left0, inv[0:256, cols])
        e2 = dot(left2, inv[256:512, cols])
        odd = dot(left1, inv[512:1024, cols])
        plus, minus = e0 + e2, e0 - e2
        odd_p, odd_n = odd[0:80], odd[80:160]
        for i, value in enumerate((plus + odd_p, minus + odd_n, plus - odd_p, minus - odd_n)):
            value = (value[0:72] * scale).reshape(9, 8, 256).astype(jnp.bfloat16)
            at = QUARTER * i + 256 * n
            out_ref[:, :, at : at + 256] = value

    for copy in pending:
        copy.wait_send()
    for i in range(8):
        pl.when(b != i)(to_owner(i).wait_send)


def on_device(records, station_row, pair_list, keep_mask, azimuth):
    forward, near, inverse = tables()
    own_pairs = azimuth.shape[1]
    bf16, f32 = jnp.bfloat16, jnp.float32
    dma = pltpu.SemaphoreType.DMA
    lagged = pl.pallas_call(
        kernel,
        out_shape=jax.ShapeDtypeStruct((9, own_pairs, NL), bf16),
        in_specs=[pl.BlockSpec(memory_space=pltpu.HBM)] * 8,
        out_specs=pl.BlockSpec(memory_space=pltpu.VMEM),
        scratch_shapes=[
            pltpu.VMEM(records.shape, bf16),
            pltpu.SMEM(station_row.shape, jnp.int32),
            pltpu.SMEM(pair_list.shape[::-1], jnp.int32),
            pltpu.VMEM(keep_mask.shape, jnp.int32),
            pltpu.VMEM(azimuth.shape, f32),
            pltpu.VMEM((24, NT), f32),
            pltpu.VMEM((QUARTER, 2 * NF), bf16),
            pltpu.VMEM((NF, NF), bf16),
            pltpu.VMEM((2 * NF, QUARTER), bf16),
            pltpu.VMEM((2, 8, 16, 128), bf16),
            pltpu.VMEM((2, 8, 16, 128), bf16),
            pltpu.VMEM((2, 8, 16, 128), bf16),
            pltpu.VMEM((2, 8, 16, 128), bf16),
            pltpu.VMEM((8, 192, 128), bf16),
            pltpu.VMEM((2, 192, 512), bf16),
            pltpu.VMEM((512, 1024), bf16),
            pltpu.VMEM((8, 80, 128), bf16),
            pltpu.VMEM((8, 80, 128), bf16),
            pltpu.VMEM((8, 80, 128), bf16),
            pltpu.VMEM((8, 80, 128), bf16),
            dma((8,)),
        ]
        + [dma((16,))] * 4
        + [dma((14,))] * 2
        + [dma((8,))] * 4,
        compiler_params=pltpu.CompilerParams(
            collective_id=0, has_side_effects=True, vmem_limit_bytes=48 << 20
        ),
        name="correlate",
    )(
        *[
            pltpu.with_memory_space_constraint(operand, pltpu.HBM)
            for operand in (records, station_row, pair_list.T, keep_mask, azimuth, forward, near, inverse)
        ]
    )
    return jnp.transpose(lagged, (1, 0, 2))


def solution(mesh):
    in_specs = (
        P("win", None, "blk", None),
        P(),
        P("blk", None),
        P("win", "blk"),
        P(None, ("blk", "win")),
    )
    out_specs = P(("blk", "win"), None, None)
    return jax.shard_map(
        on_device, mesh=mesh, in_specs=in_specs, out_specs=out_specs, check_vma=False
    )
```
